256 devices in a mesh: query: 16 (over y, x_lo, core), item: 16 (over z, x_hi).
Axes of the slice: x: 4 (x_hi: 2, x_lo: 2; x = x_hi * 2 + x_lo), y: 4, z: 8, core: 2. Of those that a mesh axis runs over, the one named last changes fastest.
Arguments:
- queries: bfloat16 [32768, 256], P('query'), may hold values from -45 to 45
- table: bfloat16 [1024, 128, 256], P('item'), may hold values from -6 to 6
- counts: int32 [1024, 128], P('item'), may hold values from 100 to 999
- lists: int32 [16, 16, 16], P('query', 'item'), may hold values from 0 to 63
- positives: int32 [32768], P('query'), may hold values from 0 to 131071
- positive_rows: bfloat16 [32768, 256], P(('query', 'item')), may hold values from -6 to 6
Outputs:
- losses: float32 [32768], P(('query', 'item'))
- query_grad: bfloat16 [32768, 256], P(('query', 'item'))
- positive_grad: bfloat16 [32768, 256], P(('query', 'item'))
- table_grad: bfloat16 [1024, 128, 256], P('item', 'query')
The draws below stay inside these ranges and needn't reach their ends.
Inputs may be any that keep to these rules, and one draw needn't show every extreme that they name: lists[g, o, c] names a block of item shard o by its index within that shard.
All inputs are finite; a program needn't handle non-finite values.
Results may differ from the reference program's by a relative error of at most 0.0051.
Values may be sent and summed in bfloat16 or wider, within the bound.
A program may use at most 128 MiB of HBM per device.

```python
import math
import jax
import jax.numpy as jnp
import numpy as np
from jax import lax

D = 256
BLOCK = 128
BLK_DEV = 64
CAP = 16
QDEV = 2048
QUERIES = 32768
BLOCKS = 1024
ITEMS = 131072
N_QUERY = 16
N_ITEM = 16


def draw_queries(key, part):
    key = jax.random.fold_in(key, 11)
    base_key = jax.random.fold_in(key, 0)
    values = jnp.clip(jax.random.normal(base_key, (QUERIES, D), jnp.float32), -6.0, 6.0)
    return values.astype(jnp.bfloat16)


def plant(result, own_key, least, top_value):
    longest = result.shape.index(max(result.shape))
    spots = []
    for shift in (0, 1):
        where = [jax.random.randint(jax.random.fold_in(own_key, axis), (), 0, length) for axis, length in enumerate(result.shape)]
        where[longest] = (where[longest] + shift) % result.shape[longest]
        spots.append(tuple(where))
    return result.at[spots[0]].set(least).at[spots[1]].set(top_value)


def levels(key, extent, cuts, low, high):
    level, own = 1.0, jax.random.fold_in(key, 6)
    for dim, parts in cuts:
        draws = jnp.exp(jax.random.uniform(jax.random.fold_in(own, dim), (parts,), jnp.float32, low / len(cuts), high / len(cuts)))
        level = level * jnp.repeat(draws, extent[dim] // parts).reshape([-1 if axis == dim else 1 for axis in range(len(extent))])
    return level


def rank_table(amount, lean):
    loads = [(1 << 20) // math.isqrt(rank ** lean) + 1 for rank in range(1, amount + 1)]
    scale = 1 + sum(loads) // (1 << 30)
    return np.cumsum(np.array([max(1, weight // scale) for weight in loads]))


def ranked_ids(own_key, shape, count, slope):
    listing = rank_table(count, slope)
    pick = jax.random.randint(jax.random.fold_in(own_key, 1), shape, 0, int(listing[count - 1]))
    standing = jnp.searchsorted(jnp.asarray(listing, jnp.int32), pick, side="right")
    return jax.random.permutation(jax.random.fold_in(own_key, 2), count)[standing].astype(jnp.int32)


def skewed_wide(stream_key, shape, amount, slope):
    loads = [min(1 << octave, amount + 1 - (1 << octave)) * (1 << 20) // math.isqrt((1 << octave) ** slope) + 1 for octave in range((amount + 1).bit_length()) if 1 << octave <= amount]
    width = 1 + sum(loads) // (1 << 30)
    listing = np.cumsum(np.array([max(1, weight // width) for weight in loads]))
    pick = jax.random.randint(jax.random.fold_in(stream_key, 1), shape, 0, int(listing[len(loads) - 1]))
    start = jnp.left_shift(1, jnp.searchsorted(jnp.asarray(listing, jnp.int32), pick, side="right").astype(jnp.int32))
    rank = start - 1 + jax.random.randint(jax.random.fold_in(stream_key, 4), shape, 0, 1 << 30) % jnp.minimum(start, amount + 1 - start)
    return jax.random.permutation(jax.random.fold_in(stream_key, 2), amount)[rank].astype(jnp.int32)


def centred(stream_key, shape, spread, reach, cuts=(), kind=jnp.bfloat16):
    drawn = jax.random.normal(stream_key, shape, jnp.float32) * spread
    if len(cuts) > 0:
        drawn = levels(stream_key, shape, cuts, -0.22, 0.18) * drawn
    return jnp.clip(drawn, min=-reach, max=reach).astype(kind)


def setup_inputs(seed: int = 0) -> dict:
    streams_of = jax.random.split(jax.random.key(seed), 7)
    return {
        "queries": draw_queries(jax.random.fold_in(streams_of[6], 71), 0),
        "table": centred(streams_of[1], (BLOCKS, BLOCK, D), 1.0, 6.0, ((0, 16),)),
        "counts": plant(jax.random.randint(streams_of[2], (BLOCKS, BLOCK), 100, 1000), jax.random.fold_in(streams_of[2], 1), 100, 999).astype(jnp.int32),
        "lists": plant(ranked_ids(streams_of[3], (N_QUERY, N_ITEM, CAP), BLK_DEV, 2), jax.random.fold_in(streams_of[3], 3), 0, BLK_DEV - 1).astype(jnp.int32),
        "positives": plant(skewed_wide(streams_of[4], (QUERIES,), ITEMS, 2), jax.random.fold_in(streams_of[4], 3), 0, ITEMS - 1).astype(jnp.int32),
        "positive_rows": centred(streams_of[5], (QUERIES, D), 1.0, 6.0, ((0, 256),)),
    }


score_scale = 0.125


def reference(queries, table, counts, lists, positives, positive_rows):
    item_logc = jnp.log(counts.astype(jnp.float32))
    pos_logc = jnp.log(counts.reshape(-1)[positives].astype(jnp.float32)).astype(jnp.bfloat16)
    pos_logc_f = pos_logc.astype(jnp.float32)
    base = jnp.arange(N_ITEM, dtype=jnp.int32)[:, None] * BLK_DEV

    def group_step(carry, group):
        pos_acc, table_acc = carry
        start = (group * QDEV).astype(jnp.int32)
        qrows = lax.dynamic_slice_in_dim(queries, start, QDEV, 0)
        own_rows = lax.dynamic_slice_in_dim(positive_rows, start, QDEV, 0)
        own_logc = lax.dynamic_slice_in_dim(pos_logc_f, start, QDEV, 0)
        listed = lax.dynamic_index_in_dim(lists, group, 0, keepdims=False)
        ids = (base + listed).reshape(-1).astype(jnp.int32)
        keys = table[ids].reshape(-1, D)
        key_logc = item_logc[ids].reshape(-1)
        sampled = score_scale * jnp.dot(qrows, keys.T, preferred_element_type=jnp.float32) - key_logc[None, :]
        inbatch = score_scale * jnp.dot(qrows, positive_rows.T, preferred_element_type=jnp.float32) - pos_logc_f[None, :]
        top = jnp.maximum(jnp.max(sampled, axis=1), jnp.max(inbatch, axis=1))
        total = jnp.sum(jnp.exp(sampled - top[:, None]), axis=1) + jnp.sum(jnp.exp(inbatch - top[:, None]), axis=1)
        lse = top + jnp.log(total)
        label = score_scale * jnp.sum(qrows.astype(jnp.float32) * own_rows.astype(jnp.float32), axis=1) - own_logc
        losses = lse - label
        p_s = jnp.exp(sampled - lse[:, None]).astype(jnp.bfloat16)
        p_i = jnp.exp(inbatch - lse[:, None]).astype(jnp.bfloat16)
        qgrad = score_scale * (jnp.dot(p_s, keys, preferred_element_type=jnp.float32) + jnp.dot(p_i, positive_rows, preferred_element_type=jnp.float32) - own_rows.astype(jnp.float32))
        pos_acc = pos_acc + score_scale * jnp.dot(p_i.T, qrows, preferred_element_type=jnp.float32)
        block_term = score_scale * jnp.dot(p_s.T, qrows, preferred_element_type=jnp.float32)
        table_acc = table_acc.at[ids].add(block_term.reshape(-1, BLOCK, D))
        return (pos_acc, table_acc), (losses, qgrad.astype(jnp.bfloat16))

    start_carry = (jnp.zeros((QUERIES, D), jnp.float32), jnp.zeros((BLOCKS, BLOCK, D), jnp.float32))
    (pos_acc, table_acc), (losses, qgrad) = lax.scan(group_step, start_carry, jnp.arange(N_QUERY, dtype=jnp.int32))
    positive_grad = (pos_acc - score_scale * queries.astype(jnp.float32)).astype(jnp.bfloat16)
    return losses.reshape(-1), qgrad.reshape(QUERIES, D), positive_grad, table_acc.astype(jnp.bfloat16)
```

```python
import functools

import jax
import jax.numpy as jnp
from jax import lax
from jax.experimental import pallas as pl
from jax.experimental.pallas import tpu as pltpu
from jax.sharding import PartitionSpec as P

MESH = pl.DeviceIdType.MESH
F32, BF16, I32 = jnp.float32, jnp.bfloat16, jnp.int32
LOG2E = 1.4426950408889634
LN2 = 0.6931471805599453
SCALE = 0.125
TQ = 256
KC = 256
KG = 512


def iota(shape, dim):
    return lax.broadcasted_iota(I32, shape, dim)


def kernel(
    nq,
    ni,
    table_hbm,
    q_ref,
    counts_ref,
    lists_ref,
    pos_ref,
    rows_ref,
    loss_ref,
    qg_ref,
    pg_ref,
    tg_ref,
    table_v,
    keys_s,
    keys_i,
    lc_s,
    lc_i,
    e_s,
    e_i,
    s_a,
    s_b,
    m_a,
    m_b,
    mx_s,
    mx_i,
    sm_s,
    sm_i,
    g_s,
    g_i,
    wq_s,
    wq_i,
    tp,
    cnt_send,
    cnt_recv,
    log_send,
    log_recv,
    key_send,
    key_recv,
    stat_send,
    stat_recv,
    lse_send,
    lse_recv,
    b_send,
    b_recv,
    c_send,
    c_recv,
    d_send,
    d_recv,
    hot,
    table_sem,
    ssem,
    rsem,
):
    qi, ii = lax.axis_index("query"), lax.axis_index("item")
    nblk, block, width = table_v.shape
    cap = lists_ref.shape[2]
    nqry = q_ref.shape[0]
    sl = rows_ref.shape[0]
    per = block // nq
    dest = cap * per
    nk = keys_s.shape[0]
    ntile = nqry // TQ

    def to(axis, me, n, src, dst, x):
        def copy(peer, slot):
            return pltpu.make_async_remote_copy(
                src_ref=src(peer),
                dst_ref=dst.at[slot],
                send_sem=ssem.at[x, peer],
                recv_sem=rsem.at[x, slot],
                device_id={axis: peer},
                device_id_type=MESH,
            )

        def each(act):
            def step(off, _):
                act(lax.rem(me + off, n))
                return 0

            lax.fori_loop(1, n, step, 0)

        class X:
            start_to = staticmethod(lambda p: copy(p, me).start())
            start = staticmethod(lambda: each(X.start_to))
            wait_recv = staticmethod(lambda: each(lambda p: copy(p, p).wait_recv()))
            wait_send = staticmethod(lambda: each(lambda p: copy(p, me).wait_send()))

        return X

    def rows_of(ref, n):
        return lambda p: ref.at[pl.ds(pl.multiple_of(p * n, n), n)]

    x_row = to("query", qi, nq, lambda p: rows_ref, keys_i, 0)
    x_cnt = to("item", ii, ni, lambda p: cnt_send.at[p], cnt_recv, 1)
    x_log = to("query", qi, nq, lambda p: log_send, log_recv, 2)
    x_key = to("query", qi, nq, lambda p: key_send, key_recv, 3)
    x_stat = to("item", ii, ni, lambda p: stat_send.at[p], stat_recv, 4)
    x_lse = to("item", ii, ni, lambda p: lse_send, lse_recv, 5)
    x_b = to("item", ii, ni, lambda p: b_send.at[p], b_recv, 6)
    x_c = to("query", qi, nq, lambda p: c_send.at[p], c_recv, 7)
    x_d = to("query", qi, nq, lambda p: d_send.at[p], d_recv, 8)

    table_in = pltpu.make_async_copy(table_hbm, table_v, table_sem)
    table_in.start()
    barrier = pltpu.get_barrier_semaphore()

    def greet(axis, me, n):
        def step(off, _):
            pl.semaphore_signal(
                barrier, inc=1, device_id={axis: lax.rem(me + off, n)}, device_id_type=MESH
            )
            return 0

        lax.fori_loop(1, n, step, 0)

    greet("query", qi, nq)
    greet("item", ii, ni)

    lane = iota((8, dest), 1)
    lane_c, lane_r = lane // per, lane % per
    lane_key = lane_r
    for c in range(cap):
        lane_key = lane_key + jnp.where(lane_c == c, lists_ref[0, 0, c] * per, 0)
    key_send[...] = lane_key
    key_recv[qi] = lane_key

    cnt = counts_ref[...]
    halves = jnp.concatenate([cnt >> 8, cnt & 255], axis=0).astype(F32)
    by_row = jnp.transpose(halves).astype(BF16)

    def count_slice(s, _):
        p = pos_ref[pl.ds(s, 1), :]
        blk = (p >> 7) - ii * nblk
        one = (iota((nblk, sl), 0) == blk).astype(F32)
        both = jnp.concatenate([one * 256.0, one], axis=0).astype(BF16)
        found = jnp.dot(by_row, both, preferred_element_type=F32)
        found = jnp.where(iota((block, sl), 0) == (p & (block - 1)), found, 0.0)
        cnt_send[s] = jnp.broadcast_to(jnp.sum(found, axis=0, keepdims=True), (8, sl))
        return 0

    lax.fori_loop(0, ni, count_slice, 0)
    cnt_recv[ii] = cnt_send[ii]
    keys_i[qi] = rows_ref[...]

    pl.semaphore_wait(barrier, nq + ni - 2)
    x_row.start()
    x_cnt.start()
    x_key.start()

    tp[...] = jnp.zeros_like(tp)
    for c in range(cap):
        row = counts_ref[pl.ds(lists_ref[0, 0, c], 1), :].astype(F32)
        tp[c : c + 1, :] = jnp.log(row) * LOG2E
    cols = jnp.transpose(tp[...])
    for c in range(cap):
        col = jnp.broadcast_to(cols[:, c : c + 1], (block, 128))
        lc_s[:, c * per : (c + 1) * per, :] = col.reshape(nq, per, 128)
    table_in.wait()
    pair = max(1, 16 // per)
    for c in range(0, cap, pair):
        parts = [
            table_v[lists_ref[0, 0, c + j]].astype(F32).reshape(nq, per, width)
            for j in range(pair)
        ]
        both = jnp.concatenate(parts, axis=1) if pair > 1 else parts[0]
        keys_s[:, c * per : (c + pair) * per, :] = both.astype(BF16)

    def chunks(ref, size):
        n, rows = ref.shape[0], ref.shape[1]
        step = max(1, min(n, size // rows))
        return [(j, j + step) for j in range(0, n, step)], rows

    def scores(keys, lc, e, mx, sm):
        spans, rows = chunks(keys, KC)

        def tile_of(t):
            return q_ref[pl.ds(pl.multiple_of(t * TQ, TQ), TQ), :]

        def both(t_new, s_new, m_new, t_old, s_old, m_old):
            if t_new is not None:
                q = tile_of(t_new)
                m8 = jnp.full((8, TQ), -jnp.inf, F32)
            if t_old is not None:
                top = jnp.max(m_old[...], axis=0, keepdims=True)
                at = pl.ds(pl.multiple_of(t_old * TQ, TQ), TQ)
                s8 = jnp.zeros((8, TQ), F32)
            for lo, hi in spans:
                n = (hi - lo) * rows
                if t_new is not None:
                    k = keys[lo:hi].reshape(n, width)
                    d = lax.dot_general(
                        k, q, (((1,), (1,)), ((), ())), preferred_element_type=F32
                    )
                    c = lc[lo:hi].reshape(n, 128)
                    s = d * (SCALE * LOG2E) - jnp.concatenate([c] * (TQ // 128), axis=1)
                    s_new[lo * rows : hi * rows, :] = s
                    m8 = jnp.maximum(m8, jnp.max(s.reshape(n // 8, 8, TQ), axis=0))
                if t_old is not None:
                    x = jnp.exp2(s_old[lo * rows : hi * rows, :] - top)
                    s8 = s8 + jnp.sum(x.reshape(n // 8, 8, TQ), axis=0)
                    e[lo * rows : hi * rows, at] = x.astype(BF16)
            if t_new is not None:
                m_new[...] = m8
            if t_old is not None:
                mx[:, at] = top
                sm[:, at] = jnp.sum(s8, axis=0, keepdims=True)

        both(0, s_a, m_a, None, None, None)

        def pair_of_tiles(u, _):
            both(2 * u + 1, s_b, m_b, 2 * u, s_a, m_a)
            both(2 * u + 2, s_a, m_a, 2 * u + 1, s_b, m_b)
            return 0

        lax.fori_loop(0, ntile // 2 - 1, pair_of_tiles, 0)
        both(ntile - 1, s_b, m_b, ntile - 2, s_a, m_a)
        both(None, None, None, ntile - 1, s_b, m_b)

    def query_grads(keys, e, g):
        n = keys.shape[0] * keys.shape[1]

        def step(t, _):
            at = pl.ds(pl.multiple_of(t * TQ, TQ), TQ)
            g[at, :] = lax.dot_general(
                e[:, at],
                keys[...].reshape(n, width),
                (((0,), (0,)), ((), ())),
                preferred_element_type=F32,
            )
            return 0

        lax.fori_loop(0, ntile, step, 0)

    scores(keys_s, lc_s, e_s, mx_s, sm_s)

    x_cnt.wait_recv()
    total = cnt_recv[0]
    for o in range(1, ni):
        total = total + cnt_recv[o]
    mine_logc = jnp.log(total).astype(BF16).astype(F32)
    log_send[...] = mine_logc
    log_recv[qi] = mine_logc
    x_log.start()
    query_grads(keys_s, e_s, g_s)

    x_log.wait_recv()
    for g in range(nq):
        tp[g : g + 1, :] = log_recv[g, 0:1, :] * LOG2E
    cols = jnp.transpose(tp[...])
    for g in range(nq):
        lc_i[g] = jnp.broadcast_to(cols[:, g : g + 1], (sl, 128))
    x_row.wait_recv()
    scores(keys_i, lc_i, e_i, mx_i, sm_i)

    row8 = iota((8, sl), 0)
    for o in range(ni):
        at = slice(o * sl, (o + 1) * sl)
        top = jnp.maximum(mx_s[:, at], mx_i[:, at])
        part = sm_s[:, at] * jnp.exp2(mx_s[:, at] - top) + sm_i[:, at] * jnp.exp2(
            mx_i[:, at] - top
        )
        stat_send[o] = jnp.where(row8 == 0, top, part)
    stat_recv[ii] = stat_send[ii]
    x_stat.start()
    query_grads(keys_i, e_i, g_i)
    x_stat.wait_recv()
    top = stat_recv[0, 0:1, :]
    for o in range(1, ni):
        top = jnp.maximum(top, stat_recv[o, 0:1, :])
    part = jnp.zeros((1, sl), F32)
    for o in range(ni):
        part = part + stat_recv[o, 1:2, :] * jnp.exp2(stat_recv[o, 0:1, :] - top)
    lse2 = top + jnp.log(part) * LOG2E
    lse_send[...] = jnp.broadcast_to(lse2, (8, sl))
    lse_recv[ii] = lse_send[...]
    x_lse.start()

    mine = pl.ds(pl.multiple_of(ii * sl, sl), sl)
    q_mine = q_ref[mine, :].astype(F32)
    r_mine = rows_ref[...].astype(F32)
    label = SCALE * jnp.sum(q_mine * r_mine, axis=1, keepdims=True)
    label = jnp.sum(
        jnp.where(iota((sl, sl), 0) == iota((sl, sl), 1), label, 0.0), axis=0, keepdims=True
    )
    loss_ref[...] = lse2 * LN2 - (label - mine_logc[0:1, :])

    x_key.wait_recv()
    for g in range(nq):
        want = iota((nblk * per, dest), 0)
        hot[:, g * dest : (g + 1) * dest] = jnp.where(
            want == key_recv[g, 0:1, :], 1.0, 0.0
        ).astype(BF16)

    x_lse.wait_recv()
    for o in range(ni):
        at = slice(o * sl, (o + 1) * sl)
        lse = lse_recv[o, 0:1, :]
        tp[o : o + 1, :] = jnp.exp2(mx_s[:, at] - lse) * SCALE
        tp[ni + o : ni + o + 1, :] = jnp.exp2(mx_i[:, at] - lse) * SCALE
    cols = jnp.transpose(tp[...])
    for o in range(ni):
        at = slice(o * sl, (o + 1) * sl)
        w_s, w_i = cols[:, o : o + 1], cols[:, ni + o : ni + o + 1]
        q = q_ref[at, :].astype(F32)
        wq_s[at, :] = (q * w_s).astype(BF16)
        wq_i[at, :] = (q * w_i).astype(BF16)
        b_send[o] = (g_s[at, :] * w_s + g_i[at, :] * w_i).astype(BF16)
    x_b.start()

    def key_grads(e, wq, out, start, me):
        n, rows = out.shape[0], out.shape[1]
        step = max(1, min(n, KG // rows))

        def one(j, _):
            at = pl.ds(pl.multiple_of(j * step * rows, step * rows), step * rows)
            k = jnp.dot(e[at, :], wq[...], preferred_element_type=F32)
            k = k.astype(BF16).reshape(step, rows, width)
            for h in range(step):
                p = j * step + h
                out[p] = k[h]

                @pl.when(p != me)
                def _():
                    start(p)

            return 0

        lax.fori_loop(0, n // step, one, 0)

    key_grads(e_s, wq_s, d_send, x_d.start_to, qi)
    d_recv[qi] = d_send[qi]
    key_grads(e_i, wq_i, c_send, x_c.start_to, qi)
    c_recv[qi] = c_send[qi]
    b_recv[ii] = b_send[ii]

    def added(ref, n):
        def step(o, acc):
            return acc + ref[o].astype(F32)

        return lax.fori_loop(0, n, step, jnp.zeros((sl, width), F32))

    x_b.wait_recv()
    qg_ref[...] = (added(b_recv, ni) - SCALE * r_mine).astype(BF16)
    x_d.wait_recv()
    grads = jnp.dot(
        hot[...], d_recv[...].reshape(nq * dest, width), preferred_element_type=F32
    )
    tg_ref[...] = grads.reshape(nblk, per, width).astype(BF16)
    x_c.wait_recv()
    pg_ref[...] = (added(c_recv, nq) - SCALE * q_mine).astype(BF16)

    for x in (x_row, x_cnt, x_log, x_key, x_stat, x_lse, x_b, x_c, x_d):
        x.wait_send()


def solution(mesh):
    nq, ni = mesh.shape["query"], mesh.shape["item"]

    def step(queries, table, counts, lists, positives, positive_rows):
        nblk, block, width = table.shape
        nqry, sl, cap = queries.shape[0], positive_rows.shape[0], lists.shape[2]
        per = block // nq
        dest = cap * per
        nk_s, nk_i = nq * dest, nq * sl
        most = max(nk_s, nk_i)
        vm, dma = pltpu.VMEM, pltpu.SemaphoreType.DMA
        whole = pl.BlockSpec(memory_space=vm)
        loss, qg, pg, tg = pl.pallas_call(
            functools.partial(kernel, nq, ni),
            out_shape=(
                jax.ShapeDtypeStruct((1, sl), F32),
                jax.ShapeDtypeStruct((sl, width), BF16),
                jax.ShapeDtypeStruct((sl, width), BF16),
                jax.ShapeDtypeStruct((nblk, per, width), BF16),
            ),
            in_specs=[
                pl.BlockSpec(memory_space=pl.ANY),
                whole,
                whole,
                pl.BlockSpec(memory_space=pltpu.SMEM),
                whole,
                whole,
            ],
            out_specs=[whole] * 4,
            scratch_shapes=[
                vm((nblk, block, width), BF16),
                vm((nq, dest, width), BF16),
                vm((nq, sl, width), BF16),
                vm((nq, dest, 128), F32),
                vm((nq, sl, 128), F32),
                vm((nk_s, nqry), BF16),
                vm((nk_i, nqry), BF16),
                vm((most, TQ), F32),
                vm((most, TQ), F32),
                vm((8, TQ), F32),
                vm((8, TQ), F32),
                vm((1, nqry), F32),
                vm((1, nqry), F32),
                vm((1, nqry), F32),
                vm((1, nqry), F32),
                vm((nqry, width), F32),
                vm((nqry, width), F32),
                vm((nqry, width), BF16),
                vm((nqry, width), BF16),
                vm((128, 128), F32),
                vm((ni, 8, sl), F32),
                vm((ni, 8, sl), F32),
                vm((8, sl), F32),
                vm((nq, 8, sl), F32),
                vm((8, dest), I32),
                vm((nq, 8, dest), I32),
                vm((ni, 8, sl), F32),
                vm((ni, 8, sl), F32),
                vm((8, sl), F32),
                vm((ni, 8, sl), F32),
                vm((ni, sl, width), BF16),
                vm((ni, sl, width), BF16),
                vm((nq, sl, width), BF16),
                vm((nq, sl, width), BF16),
                vm((nq, dest, width), BF16),
                vm((nq, dest, width), BF16),
                vm((nblk * per, nq * dest), BF16),
                dma,
                dma((9, max(nq, ni))),
                dma((9, max(nq, ni))),
            ],
            compiler_params=pltpu.CompilerParams(
                collective_id=0, has_side_effects=True, vmem_limit_bytes=60 << 20
            ),
        )(table, queries, counts, lists, positives.reshape(-1, 128), positive_rows)
        return loss.reshape(sl), qg, pg, tg

    return jax.shard_map(
        step,
        mesh=mesh,
        in_specs=(
            P("query", None),
            P("item", None, None),
            P("item", None),
            P("query", "item", None),
            P("query"),
            P(("query", "item"), None),
        ),
        out_specs=(
            P(("query", "item")),
            P(("query", "item"), None),
            P(("query", "item"), None),
            P("item", "query", None),
        ),
        check_vma=False,
    )
```

```python
import functools

import jax
import jax.numpy as jnp
from jax import lax
from jax.experimental import pallas as pl
from jax.experimental.pallas import tpu as pltpu
from jax.sharding import PartitionSpec as P

MESH = pl.DeviceIdType.MESH
F32, BF16, I32 = jnp.float32, jnp.bfloat16, jnp.int32
LOG2E = 1.4426950408889634
LN2 = 0.6931471805599453
SCALE = 0.125
TQ = 256
KC = 256
KG = 512


def iota(shape, dim):
    return lax.broadcasted_iota(I32, shape, dim)


def kernel(
    nq,
    ni,
    table_hbm,
    q_hbm,
    counts_hbm,
    lists_hbm,
    pos_hbm,
    rows_hbm,
    loss_ref,
    qg_ref,
    pg_ref,
    tg_ref,
    table_v,
    q_ref,
    counts_ref,
    lists_ref,
    pos_ref,
    rows_ref,
    keys_s,
    keys_i,
    lc_s,
    lc_i,
    e_s,
    e_i,
    s_a,
    s_b,
    m_a,
    m_b,
    mx_s,
    mx_i,
    sm_s,
    sm_i,
    g_s,
    g_i,
    wq_s,
    wq_i,
    tp,
    cnt_send,
    cnt_recv,
    log_send,
    log_recv,
    key_send,
    key_recv,
    stat_send,
    stat_recv,
    lse_send,
    lse_recv,
    ring_send,
    ring_recv,
    half_send,
    half_recv,
    core_send,
    core_recv,
    c_send,
    c_recv,
    d_send,
    d_recv,
    hot,
    in_sem,
    ssem,
    rsem,
    ring_ssem,
    ring_rsem,
):
    qi, ii = lax.axis_index("query"), lax.axis_index("item")
    nblk, block, width = table_v.shape
    cap = lists_ref.shape[2]
    nqry = q_ref.shape[0]
    sl = rows_ref.shape[0]
    per = block // nq
    dest = cap * per
    nk = keys_s.shape[0]
    ntile = nqry // TQ
    nchip, nz = nq // 2, ni // 2
    chip, core = qi // 2, lax.rem(qi, 2)
    twin = qi + 1 - 2 * core
    z, xh = ii // 2, lax.rem(ii, 2)
    mirror = ii + 1 - 2 * xh
    reach = nz // 2

    def to(axis, me, n, src, dst, x):
        def copy(peer, slot):
            return pltpu.make_async_remote_copy(
                src_ref=src(peer),
                dst_ref=dst.at[slot],
                send_sem=ssem.at[x, peer],
                recv_sem=rsem.at[x, slot],
                device_id={axis: peer},
                device_id_type=MESH,
            )

        def each(act):
            def step(off, _):
                act(lax.rem(me + off, n))
                return 0

            lax.fori_loop(1, n, step, 0)

        class X:
            start_to = staticmethod(lambda p: copy(p, me).start())
            start = staticmethod(lambda: each(X.start_to))
            wait_recv = staticmethod(lambda: each(lambda p: copy(p, p).wait_recv()))
            wait_send = staticmethod(lambda: each(lambda p: copy(p, me).wait_send()))

        return X

    x_cnt = to("item", ii, ni, lambda p: cnt_send.at[p], cnt_recv, 1)
    x_log = to("query", qi, nq, lambda p: log_send, log_recv, 2)
    x_key = to("query", qi, nq, lambda p: key_send, key_recv, 3)
    x_stat = to("item", ii, ni, lambda p: stat_send.at[p], stat_recv, 4)
    x_lse = to("item", ii, ni, lambda p: lse_send, lse_recv, 5)
    x_d = to("query", qi, nq, lambda p: d_send.at[p], d_recv, 6)

    def remote(src, dst, x, s_at, r_at, axis, peer):
        return pltpu.make_async_remote_copy(
            src_ref=src,
            dst_ref=dst,
            send_sem=ssem.at[x, s_at],
            recv_sem=rsem.at[x, r_at],
            device_id={axis: peer},
            device_id_type=MESH,
        )

    def other_chips(act):
        def step(off, _):
            act(lax.rem(chip + off, nchip))
            return 0

        lax.fori_loop(1, nchip, step, 0)

    own_slot, twin_base = core * nchip + chip, (1 - core) * nchip

    def row_out(ch):
        return remote(rows_ref, keys_i.at[own_slot], 0, ch, own_slot, "query", ch * 2 + core)

    def row_twin():
        return remote(rows_ref, keys_i.at[own_slot], 7, chip, own_slot, "query", twin)

    def row_pass(ch):
        at = core * nchip + ch
        return remote(keys_i.at[at], keys_i.at[at], 7, ch, at, "query", twin)

    def row_from_twin(ch):
        at = twin_base + ch
        return remote(keys_i.at[at], keys_i.at[at], 7, ch, at, "query", twin)

    barrier = pltpu.get_barrier_semaphore()

    def greet(axis, me, n):
        def step(off, _):
            pl.semaphore_signal(
                barrier, inc=1, device_id={axis: lax.rem(me + off, n)}, device_id_type=MESH
            )
            return 0

        lax.fori_loop(1, n, step, 0)

    greet("query", qi, nq)
    greet("item", ii, ni)
    loads = [
        pltpu.make_async_copy(a, b, in_sem.at[j])
        for j, (a, b) in enumerate(
            (
                (rows_hbm, rows_ref),
                (lists_hbm, lists_ref),
                (counts_hbm, counts_ref),
                (pos_hbm, pos_ref),
                (table_hbm, table_v),
                (q_hbm, q_ref),
            )
        )
    ]
    for load in loads:
        load.start()
    for load in loads[:4]:
        load.wait()
    keys_i[own_slot] = rows_ref[...]

    lane = iota((1, dest), 1)
    lane_c, lane_r = lane // per, lane % per
    lane_key = lane_r
    for c in range(cap):
        lane_key = lane_key + jnp.where(lane_c == c, lists_ref[0, 0, c] * per, 0)
    key_send[...] = lane_key
    key_recv[qi] = lane_key

    cnt = counts_ref[...]
    halves = jnp.concatenate([cnt >> 8, cnt & 255], axis=0).astype(F32)
    by_row = jnp.transpose(halves).astype(BF16)

    def count_slice(s, _):
        p = pos_ref[pl.ds(s, 1), :]
        blk = (p >> 7) - ii * nblk
        one = (iota((nblk, sl), 0) == blk).astype(F32)
        both = jnp.concatenate([one * 256.0, one], axis=0).astype(BF16)
        found = jnp.dot(by_row, both, preferred_element_type=F32)
        found = jnp.where(iota((block, sl), 0) == (p & (block - 1)), found, 0.0)
        cnt_send[s] = jnp.sum(found, axis=0, keepdims=True)
        return 0

    lax.fori_loop(0, ni, count_slice, 0)
    cnt_recv[ii] = cnt_send[ii]

    pl.semaphore_wait(barrier, nq + ni - 2)
    row_twin().start()
    other_chips(lambda ch: row_out(ch).start())
    x_cnt.start()
    x_key.start()

    tp[...] = jnp.zeros_like(tp)
    for c in range(cap):
        row = counts_ref[pl.ds(lists_ref[0, 0, c], 1), :].astype(F32)
        tp[c : c + 1, :] = jnp.log(row) * LOG2E
    cols = jnp.transpose(tp[...])
    for c in range(cap):
        col = jnp.broadcast_to(cols[:, c : c + 1], (block, 128))
        lc_s[:, c * per : (c + 1) * per, :] = col.reshape(nq, per, 128)
    loads[4].wait()
    pair = max(1, 16 // per)
    for c in range(0, cap, pair):
        parts = [
            table_v[lists_ref[0, 0, c + j]].astype(F32).reshape(nq, per, width)
            for j in range(pair)
        ]
        both = jnp.concatenate(parts, axis=1) if pair > 1 else parts[0]
        keys_s[:, c * per : (c + pair) * per, :] = both.astype(BF16)

    def chunks(ref, size):
        n, rows = ref.shape[0], ref.shape[1]
        step = max(1, min(n, size // rows))
        return [(j, j + step) for j in range(0, n, step)], rows

    def scores(keys, lc, e, mx, sm):
        spans, rows = chunks(keys, KC)

        def tile_of(t):
            return q_ref[pl.ds(pl.multiple_of(t * TQ, TQ), TQ), :]

        def both(t_new, s_new, m_new, t_old, s_old, m_old):
            if t_new is not None:
                q = tile_of(t_new)
                m8 = jnp.full((8, TQ), -jnp.inf, F32)
            if t_old is not None:
                top = jnp.max(m_old[...], axis=0, keepdims=True)
                at = pl.ds(pl.multiple_of(t_old * TQ, TQ), TQ)
                s8 = jnp.zeros((8, TQ), F32)
            for lo, hi in spans:
                n = (hi - lo) * rows
                if t_new is not None:
                    k = keys[lo:hi].reshape(n, width)
                    d = lax.dot_general(
                        k, q, (((1,), (1,)), ((), ())), preferred_element_type=F32
                    )
                    c = lc[lo:hi].reshape(n, 128)
                    s = d * (SCALE * LOG2E) - jnp.concatenate([c] * (TQ // 128), axis=1)
                    s_new[lo * rows : hi * rows, :] = s
                    m8 = jnp.maximum(m8, jnp.max(s.reshape(n // 8, 8, TQ), axis=0))
                if t_old is not None:
                    x = jnp.exp2(s_old[lo * rows : hi * rows, :] - top)
                    s8 = s8 + jnp.sum(x.reshape(n // 8, 8, TQ), axis=0)
                    e[lo * rows : hi * rows, at] = x.astype(BF16)
            if t_new is not None:
                m_new[...] = m8
            if t_old is not None:
                mx[:, at] = top
                sm[:, at] = jnp.sum(s8, axis=0, keepdims=True)

        both(0, s_a, m_a, None, None, None)

        def pair_of_tiles(u, _):
            both(2 * u + 1, s_b, m_b, 2 * u, s_a, m_a)
            both(2 * u + 2, s_a, m_a, 2 * u + 1, s_b, m_b)
            return 0

        lax.fori_loop(0, ntile // 2 - 1, pair_of_tiles, 0)
        both(ntile - 1, s_b, m_b, ntile - 2, s_a, m_a)
        both(None, None, None, ntile - 1, s_b, m_b)

    def query_grads(keys, e, g):
        n = keys.shape[0] * keys.shape[1]

        def step(t, _):
            at = pl.ds(pl.multiple_of(t * TQ, TQ), TQ)
            g[at, :] = lax.dot_general(
                e[:, at],
                keys[...].reshape(n, width),
                (((0,), (0,)), ((), ())),
                preferred_element_type=F32,
            )
            return 0

        lax.fori_loop(0, ntile, step, 0)

    loads[5].wait()
    scores(keys_s, lc_s, e_s, mx_s, sm_s)

    x_cnt.wait_recv()
    total = cnt_recv[0]
    for o in range(1, ni):
        total = total + cnt_recv[o]
    mine_logc = jnp.log(total).astype(BF16).astype(F32)
    log_send[...] = mine_logc
    log_recv[qi] = mine_logc
    x_log.start()

    def pass_on(ch):
        remote(
            keys_i.at[core * nchip + ch],
            keys_i.at[core * nchip + ch],
            0,
            ch,
            core * nchip + ch,
            "query",
            ch * 2 + core,
        ).wait_recv()
        row_pass(ch).start()

    other_chips(pass_on)

    x_key.wait_recv()
    for g in range(nq):
        want = iota((nblk * per, dest), 0)
        hot[:, g * dest : (g + 1) * dest] = jnp.where(
            want == key_recv[g], 1.0, 0.0
        ).astype(BF16)

    x_log.wait_recv()
    for g in range(nq):
        tp[g : g + 1, :] = log_recv[g] * LOG2E
    cols = jnp.transpose(tp[...])
    for g in range(nq):
        lc_i[(g % 2) * nchip + g // 2] = jnp.broadcast_to(cols[:, g : g + 1], (sl, 128))

    def from_twin(ch, _):
        row_from_twin(ch).wait_recv()
        return 0

    lax.fori_loop(0, nchip, from_twin, 0)
    scores(keys_i, lc_i, e_i, mx_i, sm_i)

    row2 = iota((2, sl), 0)
    for o in range(ni):
        at = slice(o * sl, (o + 1) * sl)
        top = jnp.maximum(mx_s[:, at], mx_i[:, at])
        part = sm_s[:, at] * jnp.exp2(mx_s[:, at] - top) + sm_i[:, at] * jnp.exp2(
            mx_i[:, at] - top
        )
        stat_send[o] = jnp.where(row2 == 0, top, part)
    stat_recv[ii] = stat_send[ii]
    x_stat.start()
    query_grads(keys_s, e_s, g_s)
    x_stat.wait_recv()
    top = stat_recv[0, 0:1, :]
    for o in range(1, ni):
        top = jnp.maximum(top, stat_recv[o, 0:1, :])
    part = jnp.zeros((1, sl), F32)
    for o in range(ni):
        part = part + stat_recv[o, 1:2, :] * jnp.exp2(stat_recv[o, 0:1, :] - top)
    lse2 = top + jnp.log(part) * LOG2E
    lse_send[...] = lse2
    lse_recv[ii] = lse2
    x_lse.start()
    query_grads(keys_i, e_i, g_i)

    mine = pl.ds(pl.multiple_of(ii * sl, sl), sl)
    q_mine = q_ref[mine, :].astype(F32)
    r_mine = rows_ref[...].astype(F32)
    label = SCALE * jnp.sum(q_mine * r_mine, axis=1, keepdims=True)
    label = jnp.sum(
        jnp.where(iota((sl, sl), 0) == iota((sl, sl), 1), label, 0.0), axis=0, keepdims=True
    )
    loss_ref[...] = lse2 * LN2 - (label - mine_logc)

    x_lse.wait_recv()
    for o in range(ni):
        at = slice(o * sl, (o + 1) * sl)
        lse = lse_recv[o]
        tp[o : o + 1, :] = jnp.exp2(mx_s[:, at] - lse) * SCALE
        tp[ni + o : ni + o + 1, :] = jnp.exp2(mx_i[:, at] - lse) * SCALE
    cols = jnp.transpose(tp[...])
    for o in range(ni):
        at = slice(o * sl, (o + 1) * sl)
        w_s, w_i = cols[:, o : o + 1], cols[:, ni + o : ni + o + 1]
        q = q_ref[at, :].astype(F32)
        wq_s[at, :] = (q * w_s).astype(BF16)
        wq_i[at, :] = (q * w_i).astype(BF16)
        g_s[at, :] = g_s[at, :] * w_s + g_i[at, :] * w_i

    def own_part(zz, h):
        at = pl.multiple_of((zz * 2 + h) * sl, sl)
        return g_s[pl.ds(at, sl), :]

    def ring_copy(way, hop, h):
        to_z = lax.rem(z + (1 if way == 0 else nz - 1), nz)
        return pltpu.make_async_remote_copy(
            src_ref=ring_send.at[way, hop, h],
            dst_ref=ring_recv.at[way, hop, h],
            send_sem=ring_ssem.at[way, hop, h],
            recv_sem=ring_rsem.at[way, hop, h],
            device_id={"item": to_z * 2 + xh},
            device_id_type=MESH,
        )

    def travels(way, hop, h):
        return hop > 0 or h == way

    def ring_hop(hop):
        far = reach - hop
        for h in range(2):
            for way in range(2):
                if not travels(way, hop, h):
                    continue
                at = lax.rem(z + (far if way == 0 else nz - far), nz)
                val = own_part(at, h)
                if hop > 0 and travels(way, hop - 1, h):
                    ring_copy(way, hop - 1, h).wait_recv()
                    val = val + ring_recv[way, hop - 1, h].astype(F32)
                ring_send[way, hop, h] = val.astype(BF16)
                ring_copy(way, hop, h).start()

    def key_steps(e, wq, base, n, rows, use):
        step = max(1, min(n, KG // rows))

        def one(j, _):
            first = base + j * step
            at = pl.ds(pl.multiple_of(first * rows, rows), step * rows)
            k = jnp.dot(e[at, :], wq[...], preferred_element_type=F32)
            use(j, step, k.reshape(step, rows, width))
            return 0

        lax.fori_loop(0, n // step, one, 0)

    ring_hop(0)

    def send_rows(j, step, k):
        k = k.astype(BF16)
        for h in range(step):
            p = j * step + h
            d_send[p] = k[h]

            @pl.when(p != qi)
            def _():
                x_d.start_to(p)

    key_steps(e_s, wq_s, 0, nq, dest, send_rows)
    d_recv[qi] = d_send[qi]
    if reach > 1:
        ring_hop(1)

    def core_copy(ch):
        return remote(core_send.at[ch], core_recv.at[ch], 8, ch, ch, "query", twin)

    def send_twin(j, step, k):
        k = k.astype(BF16)
        for h in range(step):
            ch = j * step + h
            core_send[ch] = k[h]
            core_copy(ch).start()

    def c_copy(ch, slot):
        return remote(c_send.at[ch], c_recv.at[slot], 9, ch, slot, "query", ch * 2 + core)

    def send_chip(j, step, k):
        for h in range(step):
            ch = j * step + h
            core_copy(ch).wait_recv()
            c_send[ch] = (k[h] + core_recv[ch].astype(F32)).astype(BF16)

            @pl.when(ch != chip)
            def _():
                c_copy(ch, chip).start()

    key_steps(e_i, wq_i, twin_base, nchip, sl, send_twin)
    if reach > 2:
        ring_hop(2)
    key_steps(e_i, wq_i, core * nchip, nchip, sl, send_chip)
    c_recv[chip] = c_send[chip]
    for hop in range(3, reach):
        ring_hop(hop)

    sums = []
    for h in range(2):
        val = own_part(z, h)
        for way in range(2):
            if travels(way, reach - 1, h):
                ring_copy(way, reach - 1, h).wait_recv()
                val = val + ring_recv[way, reach - 1, h].astype(F32)
        sums.append(val)
    half_send[...] = jnp.where(xh == 0, sums[1], sums[0]).astype(BF16)
    half = remote(half_send, half_recv, 10, 0, 0, "item", mirror)
    half.start()
    mine_sum = jnp.where(xh == 0, sums[0], sums[1])
    half.wait_recv()
    qg_ref[...] = (mine_sum + half_recv[...].astype(F32) - SCALE * r_mine).astype(BF16)

    x_d.wait_recv()
    grads = jnp.dot(
        hot[...], d_recv[...].reshape(nq * dest, width), preferred_element_type=F32
    )
    tg_ref[...] = grads.reshape(nblk, per, width).astype(BF16)

    other_chips(lambda ch: c_copy(ch, ch).wait_recv())
    total = c_recv[0].astype(F32)
    for ch in range(1, nchip):
        total = total + c_recv[ch].astype(F32)
    pg_ref[...] = (total - SCALE * q_mine).astype(BF16)

    for x in (x_cnt, x_log, x_key, x_stat, x_lse, x_d):
        x.wait_send()
    row_twin().wait_send()
    half.wait_send()
    for hop in range(reach):
        for h in range(2):
            for way in range(2):
                if travels(way, hop, h):
                    ring_copy(way, hop, h).wait_send()

    def sent(ch):
        row_out(ch).wait_send()
        row_pass(ch).wait_send()
        c_copy(ch, chip).wait_send()

    other_chips(sent)

    def sent_twin(ch, _):
        core_copy(ch).wait_send()
        return 0

    lax.fori_loop(0, nchip, sent_twin, 0)


def solution(mesh):
    nq, ni = mesh.shape["query"], mesh.shape["item"]

    def step(queries, table, counts, lists, positives, positive_rows):
        nblk, block, width = table.shape
        nqry, sl, cap = queries.shape[0], positive_rows.shape[0], lists.shape[2]
        per = block // nq
        dest = cap * per
        nk_s, nk_i = nq * dest, nq * sl
        most = max(nk_s, nk_i)
        reach = ni // 4
        vm, dma = pltpu.VMEM, pltpu.SemaphoreType.DMA
        whole = pl.BlockSpec(memory_space=vm)
        loss, qg, pg, tg = pl.pallas_call(
            functools.partial(kernel, nq, ni),
            out_shape=(
                jax.ShapeDtypeStruct((1, sl), F32),
                jax.ShapeDtypeStruct((sl, width), BF16),
                jax.ShapeDtypeStruct((sl, width), BF16),
                jax.ShapeDtypeStruct((nblk, per, width), BF16),
            ),
            in_specs=[pl.BlockSpec(memory_space=pl.ANY)] * 6,
            out_specs=[whole] * 4,
            scratch_shapes=[
                vm((nblk, block, width), BF16),
                vm((nqry, width), BF16),
                vm((nblk, block), I32),
                pltpu.SMEM((1, 1, cap), I32),
                vm((ni, 128), I32),
                vm((sl, width), BF16),
                vm((nq, dest, width), BF16),
                vm((nq, sl, width), BF16),
                vm((nq, dest, 128), F32),
                vm((nq, sl, 128), F32),
                vm((nk_s, nqry), BF16),
                vm((nk_i, nqry), BF16),
                vm((most, TQ), F32),
                vm((most, TQ), F32),
                vm((8, TQ), F32),
                vm((8, TQ), F32),
                vm((1, nqry), F32),
                vm((1, nqry), F32),
                vm((1, nqry), F32),
                vm((1, nqry), F32),
                vm((nqry, width), F32),
                vm((nqry, width), F32),
                vm((nqry, width), BF16),
                vm((nqry, width), BF16),
                vm((128, 128), F32),
                vm((ni, 1, sl), F32),
                vm((ni, 1, sl), F32),
                vm((1, sl), F32),
                vm((nq, 1, sl), F32),
                vm((1, dest), I32),
                vm((nq, 1, dest), I32),
                vm((ni, 2, sl), F32),
                vm((ni, 2, sl), F32),
                vm((1, sl), F32),
                vm((ni, 1, sl), F32),
                vm((2, reach, 2, sl, width), BF16),
                vm((2, reach, 2, sl, width), BF16),
                vm((sl, width), BF16),
                vm((sl, width), BF16),
                vm((nq // 2, sl, width), BF16),
                vm((nq // 2, sl, width), BF16),
                vm((nq // 2, sl, width), BF16),
                vm((nq // 2, sl, width), BF16),
                vm((nq, dest, width), BF16),
                vm((nq, dest, width), BF16),
                vm((nblk * per, nq * dest), BF16),
                dma((6,)),
                dma((11, max(nq, ni))),
                dma((11, max(nq, ni))),
                dma((2, reach, 2)),
                dma((2, reach, 2)),
            ],
            compiler_params=pltpu.CompilerParams(
                collective_id=0, has_side_effects=True, vmem_limit_bytes=60 << 20
            ),
        )(table, queries, counts, lists, positives.reshape(-1, 128), positive_rows)
        return loss.reshape(sl), qg, pg, tg

    return jax.shard_map(
        step,
        mesh=mesh,
        in_specs=(
            P("query", None),
            P("item", None, None),
            P("item", None),
            P("query", "item", None),
            P("query"),
            P(("query", "item"), None),
        ),
        out_specs=(
            P(("query", "item")),
            P(("query", "item"), None),
            P(("query", "item"), None),
            P("item", "query", None),
        ),
        check_vma=False,
    )
```

```python
import functools

import jax
import jax.numpy as jnp
from jax import lax
from jax.experimental import pallas as pl
from jax.experimental.pallas import tpu as pltpu
from jax.sharding import PartitionSpec as P

MESH = pl.DeviceIdType.MESH
F32, BF16, I32 = jnp.float32, jnp.bfloat16, jnp.int32
LOG2E = 1.4426950408889634
LN2 = 0.6931471805599453
SCALE = 0.125
TQ = 256
KC = 256
KG = 512


def iota(shape, dim):
    return lax.broadcasted_iota(I32, shape, dim)


def kernel(
    nq,
    ni,
    table_hbm,
    q_hbm,
    counts_hbm,
    lists_hbm,
    pos_hbm,
    rows_hbm,
    loss_ref,
    qg_ref,
    pg_ref,
    tg_ref,
    table_v,
    q_ref,
    counts_ref,
    lists_ref,
    pos_ref,
    rows_ref,
    keys_s,
    keys_i,
    lc_s,
    lc_i,
    e_s,
    e_i,
    s_a,
    s_b,
    m_a,
    m_b,
    mx_s,
    mx_i,
    sm_s,
    sm_i,
    g_s,
    g_i,
    wq_s,
    wq_i,
    tp,
    cnt_send,
    cnt_recv,
    log_send,
    log_recv,
    key_send,
    key_recv,
    row_mx,
    row_sm,
    stat_send,
    stat_recv,
    pair_send,
    pair_recv,
    lse_rows,
    ring_send,
    ring_recv,
    half_send,
    half_recv,
    half_mine,
    tgrad,
    core_send,
    core_recv,
    c_send,
    c_recv,
    d_send,
    d_recv,
    hot,
    in_sem,
    ssem,
    rsem,
    ring_ssem,
    ring_rsem,
):
    qi, ii = lax.axis_index("query"), lax.axis_index("item")
    nblk, block, width = table_v.shape
    cap = lists_ref.shape[2]
    nqry = q_ref.shape[0]
    sl = rows_ref.shape[0]
    per = block // nq
    dest = cap * per
    nk = keys_s.shape[0]
    ntile = nqry // TQ
    nchip, nz = nq // 2, ni // 2
    chip, core = qi // 2, lax.rem(qi, 2)
    twin = qi + 1 - 2 * core
    z, xh = ii // 2, lax.rem(ii, 2)
    mirror = ii + 1 - 2 * xh
    reach = nz // 2

    def to(axis, me, n, src, dst, x):
        def copy(peer, slot):
            return pltpu.make_async_remote_copy(
                src_ref=src(peer),
                dst_ref=dst.at[slot],
                send_sem=ssem.at[x, peer],
                recv_sem=rsem.at[x, slot],
                device_id={axis: peer},
                device_id_type=MESH,
            )

        def each(act):
            def step(off, _):
                act(lax.rem(me + off, n))
                return 0

            lax.fori_loop(1, n, step, 0)

        class X:
            start_to = staticmethod(lambda p: copy(p, me).start())
            start = staticmethod(lambda: each(X.start_to))
            wait_from = staticmethod(lambda p: copy(p, p).wait_recv())
            wait_recv = staticmethod(lambda: each(lambda p: copy(p, p).wait_recv()))
            wait_send = staticmethod(lambda: each(lambda p: copy(p, me).wait_send()))

        return X

    x_cnt = to("item", ii, ni, lambda p: cnt_send.at[p], cnt_recv, 1)
    x_log = to("query", qi, nq, lambda p: log_send, log_recv, 2)
    x_key = to("query", qi, nq, lambda p: key_send, key_recv, 3)
    x_d = to("query", qi, nq, lambda p: d_send.at[p], d_recv, 6)

    def remote(src, dst, x, s_at, r_at, axis, peer):
        return pltpu.make_async_remote_copy(
            src_ref=src,
            dst_ref=dst,
            send_sem=ssem.at[x, s_at],
            recv_sem=rsem.at[x, r_at],
            device_id={axis: peer},
            device_id_type=MESH,
        )

    def other_chips(act):
        def step(off, _):
            act(lax.rem(chip + off, nchip))
            return 0

        lax.fori_loop(1, nchip, step, 0)

    own_slot, twin_base = core * nchip + chip, (1 - core) * nchip

    def row_out(ch):
        return remote(rows_ref, keys_i.at[own_slot], 0, ch, own_slot, "query", ch * 2 + core)

    def row_twin():
        return remote(rows_ref, keys_i.at[own_slot], 7, chip, own_slot, "query", twin)

    def row_pass(ch):
        at = core * nchip + ch
        return remote(keys_i.at[at], keys_i.at[at], 7, ch, at, "query", twin)

    def row_from_twin(ch):
        at = twin_base + ch
        return remote(keys_i.at[at], keys_i.at[at], 7, ch, at, "query", twin)

    barrier = pltpu.get_barrier_semaphore()

    def greet(axis, me, n):
        def step(off, _):
            pl.semaphore_signal(
                barrier, inc=1, device_id={axis: lax.rem(me + off, n)}, device_id_type=MESH
            )
            return 0

        lax.fori_loop(1, n, step, 0)

    greet("query", qi, nq)
    greet("item", ii, ni)
    loads = [
        pltpu.make_async_copy(a, b, in_sem.at[j])
        for j, (a, b) in enumerate(
            (
                (rows_hbm, rows_ref),
                (lists_hbm, lists_ref),
                (counts_hbm, counts_ref),
                (pos_hbm, pos_ref),
                (table_hbm, table_v),
                (q_hbm, q_ref),
            )
        )
    ]
    for load in loads:
        load.start()
    loads[0].wait()
    keys_i[own_slot] = rows_ref[...]
    pl.semaphore_wait(barrier, nq + ni - 2)
    other_chips(lambda ch: row_out(ch).start())
    row_twin().start()
    for load in loads[1:4]:
        load.wait()

    cnt = counts_ref[...]
    halves = jnp.concatenate([cnt >> 8, cnt & 255], axis=0).astype(F32)
    by_row = jnp.transpose(halves).astype(BF16)

    wide = min(4, ni)
    for o in range(0, ni, wide):
        p = jnp.concatenate([pos_ref[o + j : o + j + 1, :] for j in range(wide)], axis=1)
        blk = (p >> 7) - ii * nblk
        one = (iota((nblk, wide * sl), 0) == blk).astype(F32)
        both = jnp.concatenate([one * 256.0, one], axis=0).astype(BF16)
        found = jnp.dot(by_row, both, preferred_element_type=F32)
        found = jnp.where(iota((block, wide * sl), 0) == (p & (block - 1)), found, 0.0)
        found = jnp.sum(found, axis=0, keepdims=True)
        for j in range(wide):
            cnt_send[o + j] = found[:, j * sl : (j + 1) * sl]
    cnt_recv[ii] = cnt_send[ii]
    x_cnt.start()

    lane = iota((1, dest), 1)
    lane_c, lane_r = lane // per, lane % per
    lane_key = lane_r
    for c in range(cap):
        lane_key = lane_key + jnp.where(lane_c == c, lists_ref[0, 0, c] * per, 0)
    key_send[...] = lane_key
    key_recv[qi] = lane_key
    x_key.start()

    tp[...] = jnp.zeros_like(tp)
    for c in range(cap):
        row = counts_ref[pl.ds(lists_ref[0, 0, c], 1), :].astype(F32)
        tp[c : c + 1, :] = jnp.log(row) * LOG2E
    cols = jnp.transpose(tp[...])
    for c in range(cap):
        col = jnp.broadcast_to(cols[:, c : c + 1], (block, 128))
        lc_s[:, c * per : (c + 1) * per, :] = col.reshape(nq, per, 128)
    loads[4].wait()
    pair = max(1, 16 // per)
    for c in range(0, cap, pair):
        parts = [
            table_v[lists_ref[0, 0, c + j]].astype(F32).reshape(nq, per, width)
            for j in range(pair)
        ]
        both = jnp.concatenate(parts, axis=1) if pair > 1 else parts[0]
        keys_s[:, c * per : (c + pair) * per, :] = both.astype(BF16)

    def chunks(ref, size):
        n, rows = ref.shape[0], ref.shape[1]
        step = max(1, min(n, size // rows))
        return [(j, j + step) for j in range(0, n, step)], rows

    def scores(keys, lc, e, mx, sm, between=None):
        spans, rows = chunks(keys, KC)

        def tile_of(t):
            return q_ref[pl.ds(pl.multiple_of(t * TQ, TQ), TQ), :]

        def both(t_new, s_new, m_new, t_old, s_old, m_old):
            if t_new is not None:
                q = tile_of(t_new)
                m8 = jnp.full((8, TQ), -jnp.inf, F32)
            if t_old is not None:
                top = jnp.max(m_old[...], axis=0, keepdims=True)
                at = pl.ds(pl.multiple_of(t_old * TQ, TQ), TQ)
                s8 = jnp.zeros((8, TQ), F32)
            for lo, hi in spans:
                n = (hi - lo) * rows
                if t_new is not None:
                    k = keys[lo:hi].reshape(n, width)
                    d = lax.dot_general(
                        k, q, (((1,), (1,)), ((), ())), preferred_element_type=F32
                    )
                    c = lc[lo:hi].reshape(n, 128)
                    s = d * (SCALE * LOG2E) - jnp.concatenate([c] * (TQ // 128), axis=1)
                    s_new[lo * rows : hi * rows, :] = s
                    m8 = jnp.maximum(m8, jnp.max(s.reshape(n // 8, 8, TQ), axis=0))
                if t_old is not None:
                    x = jnp.exp2(s_old[lo * rows : hi * rows, :] - top)
                    s8 = s8 + jnp.sum(x.reshape(n // 8, 8, TQ), axis=0)
                    e[lo * rows : hi * rows, at] = x.astype(BF16)
            if t_new is not None:
                m_new[...] = m8
            if t_old is not None:
                mx[:, at] = top
                sm[:, at] = jnp.sum(s8, axis=0, keepdims=True)

        both(0, s_a, m_a, None, None, None)

        def pair_of_tiles(u, _):
            both(2 * u + 1, s_b, m_b, 2 * u, s_a, m_a)
            both(2 * u + 2, s_a, m_a, 2 * u + 1, s_b, m_b)
            return 0

        lax.fori_loop(0, ntile // 2 - 1, pair_of_tiles, 0)
        if between is not None:
            between()
        both(ntile - 1, s_b, m_b, ntile - 2, s_a, m_a)
        both(None, None, None, ntile - 1, s_b, m_b)

    def query_grads(keys, e, g, half):
        n = keys.shape[0] * keys.shape[1]
        at = slice(half * nqry // 2, (half + 1) * nqry // 2)
        g[at, :] = lax.dot_general(
            e[:, at],
            keys[...].reshape(n, width),
            (((0,), (0,)), ((), ())),
            preferred_element_type=F32,
        )

    loads[5].wait()

    def log_counts():
        x_cnt.wait_recv()
        total = cnt_recv[0]
        for o in range(1, ni):
            total = total + cnt_recv[o]
        mine_logc = jnp.log(total).astype(BF16).astype(F32)
        log_send[...] = mine_logc
        log_recv[qi] = mine_logc
        x_log.start()

    scores(keys_s, lc_s, e_s, mx_s, sm_s, log_counts)

    def pass_on(ch):
        remote(
            keys_i.at[core * nchip + ch],
            keys_i.at[core * nchip + ch],
            0,
            ch,
            core * nchip + ch,
            "query",
            ch * 2 + core,
        ).wait_recv()
        row_pass(ch).start()

    other_chips(pass_on)

    x_key.wait_recv()
    for g in range(nq):
        want = iota((nblk * per, dest), 0)
        hot[:, g * dest : (g + 1) * dest] = jnp.where(
            want == key_recv[g], 1.0, 0.0
        ).astype(BF16)

    query_grads(keys_s, e_s, g_s, 0)
    x_log.wait_recv()
    for g in range(nq):
        tp[g : g + 1, :] = log_recv[g] * LOG2E
    cols = jnp.transpose(tp[...])
    for g in range(nq):
        lc_i[(g % 2) * nchip + g // 2] = jnp.broadcast_to(cols[:, g : g + 1], (sl, 128))

    def from_twin(ch, _):
        row_from_twin(ch).wait_recv()
        return 0

    lax.fori_loop(0, nchip, from_twin, 0)
    scores(keys_i, lc_i, e_i, mx_i, sm_i)

    for o in range(ni):
        at = slice(o * sl, (o + 1) * sl)
        row_mx[o : o + 1, :] = mx_s[:, at]
        row_mx[ni + o : ni + o + 1, :] = mx_i[:, at]
        row_sm[o : o + 1, :] = sm_s[:, at]
        row_sm[ni + o : ni + o + 1, :] = sm_i[:, at]

    def met(pairs):
        top = pairs[0][0]
        for m, _ in pairs[1:]:
            top = jnp.maximum(top, m)
        return top, sum(v * jnp.exp2(m - top) for m, v in pairs)

    top, part = met(
        [(row_mx[j : j + ni, :], row_sm[j : j + ni, :]) for j in (0, ni)]
    )
    stat_send[0], stat_send[1] = top, part
    stat_recv[z, 0], stat_recv[z, 1] = top, part

    def stat_copy(zz, slot):
        return remote(stat_send, stat_recv.at[slot], 4, zz, slot, "item", zz * 2 + xh)

    def other_z(act):
        def step(off, _):
            act(lax.rem(z + off, nz))
            return 0

        lax.fori_loop(1, nz, step, 0)

    other_z(lambda zz: stat_copy(zz, z).start())
    query_grads(keys_s, e_s, g_s, 1)
    other_z(lambda zz: stat_copy(zz, zz).wait_recv())
    top, part = met([(stat_recv[j, 0], stat_recv[j, 1]) for j in range(nz)])
    pair_send[0], pair_send[1] = top, part
    stat_pair = remote(pair_send, pair_recv, 5, 0, 0, "item", mirror)
    stat_pair.start()
    query_grads(keys_i, e_i, g_i, 0)
    query_grads(keys_i, e_i, g_i, 1)
    stat_pair.wait_recv()
    top, part = met([(pair_send[0], pair_send[1]), (pair_recv[0], pair_recv[1])])
    lse_rows[...] = top + jnp.log(part) * LOG2E

    mine = pl.ds(pl.multiple_of(ii * sl, sl), sl)
    q_mine = q_ref[mine, :].astype(F32)
    r_mine = rows_ref[...].astype(F32)
    label = SCALE * jnp.sum(q_mine * r_mine, axis=1, keepdims=True)
    label = jnp.sum(
        jnp.where(iota((sl, sl), 0) == iota((sl, sl), 1), label, 0.0), axis=0, keepdims=True
    )
    loss_ref[...] = lse_rows[pl.ds(ii, 1), :] * LN2 - (label - log_send[...])

    for j in (0, ni):
        tp[j : j + ni, :] = jnp.exp2(row_mx[j : j + ni, :] - lse_rows[...]) * SCALE
    cols = jnp.transpose(tp[...])
    for o in range(ni):
        at = slice(o * sl, (o + 1) * sl)
        w_s, w_i = cols[:, o : o + 1], cols[:, ni + o : ni + o + 1]
        q = q_ref[at, :].astype(F32)
        wq_s[at, :] = (q * w_s).astype(BF16)
        wq_i[at, :] = (q * w_i).astype(BF16)
        g_s[at, :] = g_s[at, :] * w_s + g_i[at, :] * w_i

    def own_part(zz, h):
        at = pl.multiple_of((zz * 2 + h) * sl, sl)
        return g_s[pl.ds(at, sl), :]

    def ring_copy(way, hop, h):
        to_z = lax.rem(z + (1 if way == 0 else nz - 1), nz)
        return pltpu.make_async_remote_copy(
            src_ref=ring_send.at[way, hop, h],
            dst_ref=ring_recv.at[way, hop, h],
            send_sem=ring_ssem.at[way, hop, h],
            recv_sem=ring_rsem.at[way, hop, h],
            device_id={"item": to_z * 2 + xh},
            device_id_type=MESH,
        )

    def travels(way, hop, h):
        return hop > 0 or h == way

    def ring_step(late, hop):
        far = reach - hop
        for way in range(2):
            h = way if late == 0 else 1 - way
            at = lax.rem(z + (far if way == 0 else nz - far), nz)
            val = own_part(at, h)
            if hop > late:
                ring_copy(way, hop - 1, h).wait_recv()
                val = val + ring_recv[way, hop - 1, h].astype(F32)
            ring_send[way, hop, h] = val.astype(BF16)
            ring_copy(way, hop, h).start()

    ring_steps = [(late, hop) for hop in range(1, reach) for late in (1, 0) if hop > late]

    def ring_next():
        if ring_steps:
            ring_step(*ring_steps.pop(0))

    def key_steps(e, wq, base, n, rows, use, shift=0):
        step = max(1, min(n, KG // rows))

        def one(j, _):
            j = lax.rem(j + shift, n // step)
            first = base + j * step
            at = pl.ds(pl.multiple_of(first * rows, rows), step * rows)
            k = jnp.dot(e[at, :], wq[...], preferred_element_type=F32)
            use(j, step, k.reshape(step, rows, width))
            return 0

        lax.fori_loop(0, n // step, one, 0)

    ring_step(0, 0)
    if reach > 1:
        ring_step(1, 1)

    def send_rows(j, step, k):
        k = k.astype(BF16)
        for h in range(step):
            p = j * step + h
            d_send[p] = k[h]

            @pl.when(p != qi)
            def _():
                x_d.start_to(p)

    lines = 4 if nq >= 16 else 1
    line = qi // (nq // lines)
    key_steps(e_s, wq_s, 0, nq, dest, send_rows, line + 2)
    d_recv[qi] = d_send[qi]
    ring_next()

    def core_copy(ch):
        return remote(core_send.at[ch], core_recv.at[ch], 8, ch, ch, "query", twin)

    def send_twin(j, step, k):
        k = k.astype(BF16)
        for h in range(step):
            ch = j * step + h
            core_send[ch] = k[h]
            core_copy(ch).start()

    def c_copy(ch, slot):
        return remote(c_send.at[ch], c_recv.at[slot], 9, ch, slot, "query", ch * 2 + core)

    def send_chip(j, step, k):
        for h in range(step):
            ch = j * step + h
            core_copy(ch).wait_recv()
            c_send[ch] = (k[h] + core_recv[ch].astype(F32)).astype(BF16)

            @pl.when(ch != chip)
            def _():
                c_copy(ch, chip).start()

    key_steps(e_i, wq_i, twin_base, nchip, sl, send_twin)
    ring_next()
    key_steps(e_i, wq_i, core * nchip, nchip, sl, send_chip)
    c_recv[chip] = c_send[chip]
    while ring_steps:
        ring_next()

    def table_part(j):
        many = nq // lines
        first = lax.rem(line + j, lines) * many

        def arrived(k, _):
            @pl.when(first + k != qi)
            def _():
                x_d.wait_from(first + k)

            return 0

        lax.fori_loop(0, many, arrived, 0)
        at = pl.ds(pl.multiple_of(first * dest, dest), many * dest)
        got = d_recv[pl.ds(first, many)].reshape(many * dest, width)
        part = jnp.dot(hot[:, at], got, preferred_element_type=F32)
        if j > 0:
            part = part + tgrad[...]
        if j < lines - 1:
            tgrad[...] = part
        else:
            tg_ref[...] = part.reshape(nblk, per, width).astype(BF16)

    for j in range(lines // 2):
        table_part(j)
    sums = []
    for h in range(2):
        val = own_part(z, h)
        for way in range(2):
            if travels(way, reach - 1, h):
                ring_copy(way, reach - 1, h).wait_recv()
                val = val + ring_recv[way, reach - 1, h].astype(F32)
        sums.append(val)
    half_send[...] = jnp.where(xh == 0, sums[1], sums[0]).astype(BF16)
    half = remote(half_send, half_recv, 10, 0, 0, "item", mirror)
    half.start()
    half_mine[...] = jnp.where(xh == 0, sums[0], sums[1]) - SCALE * r_mine
    for j in range(lines // 2, lines):
        table_part(j)
    half.wait_recv()
    qg_ref[...] = (half_mine[...] + half_recv[...].astype(F32)).astype(BF16)

    other_chips(lambda ch: c_copy(ch, ch).wait_recv())
    total = c_recv[0].astype(F32)
    for ch in range(1, nchip):
        total = total + c_recv[ch].astype(F32)
    pg_ref[...] = (total - SCALE * q_mine).astype(BF16)

    for x in (x_cnt, x_log, x_key, x_d):
        x.wait_send()
    row_twin().wait_send()
    other_z(lambda zz: stat_copy(zz, z).wait_send())
    stat_pair.wait_send()
    half.wait_send()
    for hop in range(reach):
        for h in range(2):
            for way in range(2):
                if travels(way, hop, h):
                    ring_copy(way, hop, h).wait_send()

    def sent(ch):
        row_out(ch).wait_send()
        row_pass(ch).wait_send()
        c_copy(ch, chip).wait_send()

    other_chips(sent)

    def sent_twin(ch, _):
        core_copy(ch).wait_send()
        return 0

    lax.fori_loop(0, nchip, sent_twin, 0)


def hand_over(*refs):
    for j in range(4):
        refs[4 + j][...] = refs[j][...]


def solution(mesh):
    nq, ni = mesh.shape["query"], mesh.shape["item"]

    def step(queries, table, counts, lists, positives, positive_rows):
        nblk, block, width = table.shape
        nqry, sl, cap = queries.shape[0], positive_rows.shape[0], lists.shape[2]
        per = block // nq
        dest = cap * per
        nk_s, nk_i = nq * dest, nq * sl
        most = max(nk_s, nk_i)
        reach = ni // 4
        vm, dma = pltpu.VMEM, pltpu.SemaphoreType.DMA
        whole = pl.BlockSpec(memory_space=vm)
        loss, qg, pg, tg = pl.pallas_call(
            functools.partial(kernel, nq, ni),
            out_shape=(
                jax.ShapeDtypeStruct((1, sl), F32),
                jax.ShapeDtypeStruct((sl, width), BF16),
                jax.ShapeDtypeStruct((sl, width), BF16),
                jax.ShapeDtypeStruct((nblk, per, width), BF16),
            ),
            in_specs=[pl.BlockSpec(memory_space=pl.ANY)] * 6,
            out_specs=[whole] * 4,
            scratch_shapes=[
                vm((nblk, block, width), BF16),
                vm((nqry, width), BF16),
                vm((nblk, block), I32),
                pltpu.SMEM((1, 1, cap), I32),
                vm((ni, 128), I32),
                vm((sl, width), BF16),
                vm((nq, dest, width), BF16),
                vm((nq, sl, width), BF16),
                vm((nq, dest, 128), F32),
                vm((nq, sl, 128), F32),
                vm((nk_s, nqry), BF16),
                vm((nk_i, nqry), BF16),
                vm((most, TQ), F32),
                vm((most, TQ), F32),
                vm((8, TQ), F32),
                vm((8, TQ), F32),
                vm((1, nqry), F32),
                vm((1, nqry), F32),
                vm((1, nqry), F32),
                vm((1, nqry), F32),
                vm((nqry, width), F32),
                vm((nqry, width), F32),
                vm((nqry, width), BF16),
                vm((nqry, width), BF16),
                vm((128, 128), F32),
                vm((ni, 1, sl), F32),
                vm((ni, 1, sl), F32),
                vm((1, sl), F32),
                vm((nq, 1, sl), F32),
                vm((1, dest), I32),
                vm((nq, 1, dest), I32),
                vm((2 * ni, sl), F32),
                vm((2 * ni, sl), F32),
                vm((2, ni, sl), F32),
                vm((ni // 2, 2, ni, sl), F32),
                vm((2, ni, sl), F32),
                vm((2, ni, sl), F32),
                vm((ni, sl), F32),
                vm((2, reach, 2, sl, width), BF16),
                vm((2, reach, 2, sl, width), BF16),
                vm((sl, width), BF16),
                vm((sl, width), BF16),
                vm((sl, width), F32),
                vm((nblk * per, width), F32),
                vm((nq // 2, sl, width), BF16),
                vm((nq // 2, sl, width), BF16),
                vm((nq // 2, sl, width), BF16),
                vm((nq // 2, sl, width), BF16),
                vm((nq, dest, width), BF16),
                vm((nq, dest, width), BF16),
                vm((nblk * per, nq * dest), BF16),
                dma((6,)),
                dma((11, max(nq, ni))),
                dma((11, max(nq, ni))),
                dma((2, reach, 2)),
                dma((2, reach, 2)),
            ],
            compiler_params=pltpu.CompilerParams(
                collective_id=0, has_side_effects=True, vmem_limit_bytes=60 << 20
            ),
        )(table, queries, counts, lists, positives.reshape(-1, 128), positive_rows)
        parts = (loss, qg, pg, tg)
        loss, qg, pg, tg = pl.pallas_call(
            hand_over,
            out_shape=tuple(jax.ShapeDtypeStruct(a.shape, a.dtype) for a in parts),
        )(*parts)
        return loss.reshape(sl), qg, pg, tg

    return jax.shard_map(
        step,
        mesh=mesh,
        in_specs=(
            P("query", None),
            P("item", None, None),
            P("item", None),
            P("query", "item", None),
            P("query"),
            P(("query", "item"), None),
        ),
        out_specs=(
            P(("query", "item")),
            P(("query", "item"), None),
            P(("query", "item"), None),
            P("item", "query", None),
        ),
        check_vma=False,
    )
```

```python
import functools

import jax
import jax.numpy as jnp
from jax import lax
from jax.experimental import pallas as pl
from jax.experimental.pallas import tpu as pltpu
from jax.sharding import PartitionSpec as P

MESH = pl.DeviceIdType.MESH
F32, BF16, I32 = jnp.float32, jnp.bfloat16, jnp.int32
LOG2E = 1.4426950408889634
LN2 = 0.6931471805599453
SCALE = 0.125
TQ = 256
KC = 256
KG = 512


def iota(shape, dim):
    return lax.broadcasted_iota(I32, shape, dim)


def kernel(
    nq,
    ni,
    table_hbm,
    q_hbm,
    counts_hbm,
    lists_hbm,
    pos_hbm,
    rows_hbm,
    loss_ref,
    qg_ref,
    pg_ref,
    tg_ref,
    table_v,
    q_ref,
    counts_ref,
    lists_ref,
    pos_ref,
    rows_ref,
    keys_s,
    keys_i,
    lc_s,
    lc_i,
    e_s,
    e_i,
    s_a,
    s_b,
    m_a,
    m_b,
    mx_s,
    mx_i,
    sm_s,
    sm_i,
    g_s,
    g_i,
    wq_s,
    wq_i,
    tp,
    cnt_send,
    cnt_recv,
    log_send,
    log_recv,
    key_send,
    key_recv,
    row_mx,
    row_sm,
    stat_send,
    stat_recv,
    pair_send,
    pair_recv,
    lse_rows,
    ring_send,
    ring_recv,
    half_send,
    half_recv,
    half_mine,
    tgrad,
    core_send,
    core_recv,
    c_send,
    c_recv,
    d_send,
    d_recv,
    hot,
    in_sem,
    ssem,
    rsem,
    ring_ssem,
    ring_rsem,
):
    qi, ii = lax.axis_index("query"), lax.axis_index("item")
    nblk, block, width = table_v.shape
    cap = lists_ref.shape[2]
    nqry = q_ref.shape[0]
    sl = rows_ref.shape[0]
    per = block // nq
    dest = cap * per
    nk = keys_s.shape[0]
    ntile = nqry // TQ
    nchip, nz = nq // 2, ni // 2
    chip, core = qi // 2, lax.rem(qi, 2)
    twin = qi + 1 - 2 * core
    z, xh = ii // 2, lax.rem(ii, 2)
    mirror = ii + 1 - 2 * xh
    reach = nz // 2

    def to(axis, me, n, src, dst, x):
        def copy(peer, slot):
            return pltpu.make_async_remote_copy(
                src_ref=src(peer),
                dst_ref=dst.at[slot],
                send_sem=ssem.at[x, peer],
                recv_sem=rsem.at[x, slot],
                device_id={axis: peer},
                device_id_type=MESH,
            )

        def each(act):
            def step(off, _):
                act(lax.rem(me + off, n))
                return 0

            lax.fori_loop(1, n, step, 0)

        class X:
            start_to = staticmethod(lambda p: copy(p, me).start())
            start = staticmethod(lambda: each(X.start_to))
            wait_from = staticmethod(lambda p: copy(p, p).wait_recv())
            wait_recv = staticmethod(lambda: each(lambda p: copy(p, p).wait_recv()))
            wait_send = staticmethod(lambda: each(lambda p: copy(p, me).wait_send()))

        return X

    x_cnt = to("item", ii, ni, lambda p: cnt_send.at[p], cnt_recv, 1)
    x_log = to("query", qi, nq, lambda p: log_send, log_recv, 2)
    x_key = to("query", qi, nq, lambda p: key_send, key_recv, 3)
    x_d = to("query", qi, nq, lambda p: d_send.at[p], d_recv, 6)

    def remote(src, dst, x, s_at, r_at, axis, peer):
        return pltpu.make_async_remote_copy(
            src_ref=src,
            dst_ref=dst,
            send_sem=ssem.at[x, s_at],
            recv_sem=rsem.at[x, r_at],
            device_id={axis: peer},
            device_id_type=MESH,
        )

    def other_chips(act):
        def step(off, _):
            act(lax.rem(chip + off, nchip))
            return 0

        lax.fori_loop(1, nchip, step, 0)

    own_slot, twin_base = core * nchip + chip, (1 - core) * nchip

    def row_out(ch):
        return remote(rows_ref, keys_i.at[own_slot], 0, ch, own_slot, "query", ch * 2 + core)

    def row_twin():
        return remote(rows_ref, keys_i.at[own_slot], 7, chip, own_slot, "query", twin)

    def row_pass(ch):
        at = core * nchip + ch
        return remote(keys_i.at[at], keys_i.at[at], 7, ch, at, "query", twin)

    def row_from_twin(ch):
        at = twin_base + ch
        return remote(keys_i.at[at], keys_i.at[at], 7, ch, at, "query", twin)

    barrier = pltpu.get_barrier_semaphore()

    def greet(axis, me, n):
        def step(off, _):
            pl.semaphore_signal(
                barrier, inc=1, device_id={axis: lax.rem(me + off, n)}, device_id_type=MESH
            )
            return 0

        lax.fori_loop(1, n, step, 0)

    greet("query", qi, nq)
    greet("item", ii, ni)
    loads = [
        pltpu.make_async_copy(a, b, in_sem.at[j])
        for j, (a, b) in enumerate(
            (
                (rows_hbm, rows_ref),
                (lists_hbm, lists_ref),
                (counts_hbm, counts_ref),
                (pos_hbm, pos_ref),
                (table_hbm, table_v),
                (q_hbm, q_ref),
            )
        )
    ]
    for load in loads:
        load.start()
    loads[0].wait()
    keys_i[own_slot] = rows_ref[...]
    pl.semaphore_wait(barrier, nq + ni - 2)
    other_chips(lambda ch: row_out(ch).start())
    row_twin().start()
    for load in loads[1:4]:
        load.wait()

    cnt = counts_ref[...]
    halves = jnp.concatenate([cnt >> 8, cnt & 255], axis=0).astype(F32)
    by_row = jnp.transpose(halves).astype(BF16)

    wide = min(4, ni)
    for o in range(0, ni, wide):
        p = jnp.concatenate([pos_ref[o + j : o + j + 1, :] for j in range(wide)], axis=1)
        blk = (p >> 7) - ii * nblk
        one = (iota((nblk, wide * sl), 0) == blk).astype(F32)
        both = jnp.concatenate([one * 256.0, one], axis=0).astype(BF16)
        found = jnp.dot(by_row, both, preferred_element_type=F32)
        found = jnp.where(iota((block, wide * sl), 0) == (p & (block - 1)), found, 0.0)
        found = jnp.sum(found, axis=0, keepdims=True)
        for j in range(wide):
            cnt_send[o + j] = found[:, j * sl : (j + 1) * sl]
    cnt_recv[ii] = cnt_send[ii]
    x_cnt.start()

    lane = iota((1, dest), 1)
    lane_c, lane_r = lane // per, lane % per
    lane_key = lane_r
    for c in range(cap):
        lane_key = lane_key + jnp.where(lane_c == c, lists_ref[0, 0, c] * per, 0)
    key_send[...] = lane_key
    key_recv[qi] = lane_key
    x_key.start()

    tp[...] = jnp.zeros_like(tp)
    for c in range(cap):
        row = counts_ref[pl.ds(lists_ref[0, 0, c], 1), :].astype(F32)
        tp[c : c + 1, :] = jnp.log(row) * LOG2E
    cols = jnp.transpose(tp[...])
    for c in range(cap):
        col = jnp.broadcast_to(cols[:, c : c + 1], (block, 128))
        lc_s[:, c * per : (c + 1) * per, :] = col.reshape(nq, per, 128)
    loads[4].wait()
    pair = max(1, 16 // per)
    for c in range(0, cap, pair):
        parts = [
            table_v[lists_ref[0, 0, c + j]].astype(F32).reshape(nq, per, width)
            for j in range(pair)
        ]
        both = jnp.concatenate(parts, axis=1) if pair > 1 else parts[0]
        keys_s[:, c * per : (c + pair) * per, :] = both.astype(BF16)

    def chunks(ref, size):
        n, rows = ref.shape[0], ref.shape[1]
        step = max(1, min(n, size // rows))
        return [(j, j + step) for j in range(0, n, step)], rows

    def scores(keys, lc, e, mx, sm, between=None):
        spans, rows = chunks(keys, KC)

        def tile_of(t):
            return q_ref[pl.ds(pl.multiple_of(t * TQ, TQ), TQ), :]

        def both(t_new, s_new, m_new, t_old, s_old, m_old):
            if t_new is not None:
                q = tile_of(t_new)
                m8 = jnp.full((8, TQ), -jnp.inf, F32)
            if t_old is not None:
                top = jnp.max(m_old[...], axis=0, keepdims=True)
                at = pl.ds(pl.multiple_of(t_old * TQ, TQ), TQ)
                s8 = jnp.zeros((8, TQ), F32)
            for lo, hi in spans:
                n = (hi - lo) * rows
                if t_new is not None:
                    k = keys[lo:hi].reshape(n, width)
                    d = lax.dot_general(
                        k, q, (((1,), (1,)), ((), ())), preferred_element_type=F32
                    )
                    c = lc[lo:hi].reshape(n, 128)
                    s = d * (SCALE * LOG2E) - jnp.concatenate([c] * (TQ // 128), axis=1)
                    s_new[lo * rows : hi * rows, :] = s
                    m8 = jnp.maximum(m8, jnp.max(s.reshape(n // 8, 8, TQ), axis=0))
                if t_old is not None:
                    x = jnp.exp2(s_old[lo * rows : hi * rows, :] - top)
                    s8 = s8 + jnp.sum(x.reshape(n // 8, 8, TQ), axis=0)
                    e[lo * rows : hi * rows, at] = x.astype(BF16)
            if t_new is not None:
                m_new[...] = m8
            if t_old is not None:
                mx[:, at] = top
                sm[:, at] = jnp.sum(s8, axis=0, keepdims=True)

        both(0, s_a, m_a, None, None, None)

        def pair_of_tiles(u, _):
            both(2 * u + 1, s_b, m_b, 2 * u, s_a, m_a)
            both(2 * u + 2, s_a, m_a, 2 * u + 1, s_b, m_b)
            return 0

        lax.fori_loop(0, ntile // 2 - 1, pair_of_tiles, 0)
        if between is not None:
            between()
        both(ntile - 1, s_b, m_b, ntile - 2, s_a, m_a)
        both(None, None, None, ntile - 1, s_b, m_b)

    def query_grads(keys, e, g, half):
        n = keys.shape[0] * keys.shape[1]
        at = slice(half * nqry // 2, (half + 1) * nqry // 2)
        g[at, :] = lax.dot_general(
            e[:, at],
            keys[...].reshape(n, width),
            (((0,), (0,)), ((), ())),
            preferred_element_type=F32,
        )

    loads[5].wait()

    def log_counts():
        x_cnt.wait_recv()
        total = cnt_recv[0]
        for o in range(1, ni):
            total = total + cnt_recv[o]
        mine_logc = jnp.log(total).astype(BF16).astype(F32)
        log_send[...] = mine_logc
        log_recv[qi] = mine_logc
        x_log.start()

    scores(keys_s, lc_s, e_s, mx_s, sm_s, log_counts)

    def pass_on(ch):
        remote(
            keys_i.at[core * nchip + ch],
            keys_i.at[core * nchip + ch],
            0,
            ch,
            core * nchip + ch,
            "query",
            ch * 2 + core,
        ).wait_recv()
        row_pass(ch).start()

    other_chips(pass_on)

    x_key.wait_recv()
    for g in range(nq):
        want = iota((nblk * per, dest), 0)
        hot[:, g * dest : (g + 1) * dest] = jnp.where(
            want == key_recv[g], 1.0, 0.0
        ).astype(BF16)

    query_grads(keys_s, e_s, g_s, 0)
    x_log.wait_recv()
    for g in range(nq):
        tp[g : g + 1, :] = log_recv[g] * LOG2E
    cols = jnp.transpose(tp[...])
    for g in range(nq):
        lc_i[(g % 2) * nchip + g // 2] = jnp.broadcast_to(cols[:, g : g + 1], (sl, 128))

    def from_twin(ch, _):
        row_from_twin(ch).wait_recv()
        return 0

    lax.fori_loop(0, nchip, from_twin, 0)
    scores(keys_i, lc_i, e_i, mx_i, sm_i)

    for o in range(ni):
        at = slice(o * sl, (o + 1) * sl)
        row_mx[o : o + 1, :] = mx_s[:, at]
        row_mx[ni + o : ni + o + 1, :] = mx_i[:, at]
        row_sm[o : o + 1, :] = sm_s[:, at]
        row_sm[ni + o : ni + o + 1, :] = sm_i[:, at]

    def met(pairs):
        top = pairs[0][0]
        for m, _ in pairs[1:]:
            top = jnp.maximum(top, m)
        return top, sum(v * jnp.exp2(m - top) for m, v in pairs)

    top, part = met(
        [(row_mx[j : j + ni, :], row_sm[j : j + ni, :]) for j in (0, ni)]
    )
    stat_send[0], stat_send[1] = top, part
    stat_recv[z, 0], stat_recv[z, 1] = top, part

    def stat_copy(zz, slot):
        return remote(stat_send, stat_recv.at[slot], 4, zz, slot, "item", zz * 2 + xh)

    def other_z(act):
        def step(off, _):
            act(lax.rem(z + off, nz))
            return 0

        lax.fori_loop(1, nz, step, 0)

    other_z(lambda zz: stat_copy(zz, z).start())
    query_grads(keys_s, e_s, g_s, 1)
    other_z(lambda zz: stat_copy(zz, zz).wait_recv())
    top, part = met([(stat_recv[j, 0], stat_recv[j, 1]) for j in range(nz)])
    pair_send[0], pair_send[1] = top, part
    stat_pair = remote(pair_send, pair_recv, 5, 0, 0, "item", mirror)
    stat_pair.start()
    query_grads(keys_i, e_i, g_i, 0)
    query_grads(keys_i, e_i, g_i, 1)
    stat_pair.wait_recv()
    top, part = met([(pair_send[0], pair_send[1]), (pair_recv[0], pair_recv[1])])
    lse_rows[...] = top + jnp.log(part) * LOG2E

    mine = pl.ds(pl.multiple_of(ii * sl, sl), sl)
    q_mine = q_ref[mine, :].astype(F32)
    r_mine = rows_ref[...].astype(F32)
    label = SCALE * jnp.sum(q_mine * r_mine, axis=1, keepdims=True)
    label = jnp.sum(
        jnp.where(iota((sl, sl), 0) == iota((sl, sl), 1), label, 0.0), axis=0, keepdims=True
    )
    loss_ref[...] = lse_rows[pl.ds(ii, 1), :] * LN2 - (label - log_send[...])

    for j in (0, ni):
        tp[j : j + ni, :] = jnp.exp2(row_mx[j : j + ni, :] - lse_rows[...]) * SCALE
    cols = jnp.transpose(tp[...])
    for o in range(ni):
        at = slice(o * sl, (o + 1) * sl)
        w_s, w_i = cols[:, o : o + 1], cols[:, ni + o : ni + o + 1]
        q = q_ref[at, :].astype(F32)
        wq_s[at, :] = (q * w_s).astype(BF16)
        wq_i[at, :] = (q * w_i).astype(BF16)
        g_s[at, :] = g_s[at, :] * w_s + g_i[at, :] * w_i

    def own_part(zz, h):
        at = pl.multiple_of((zz * 2 + h) * sl, sl)
        return g_s[pl.ds(at, sl), :]

    def ring_copy(way, hop, h):
        to_z = lax.rem(z + (1 if way == 0 else nz - 1), nz)
        return pltpu.make_async_remote_copy(
            src_ref=ring_send.at[way, hop, h],
            dst_ref=ring_recv.at[way, hop, h],
            send_sem=ring_ssem.at[way, hop, h],
            recv_sem=ring_rsem.at[way, hop, h],
            device_id={"item": to_z * 2 + xh},
            device_id_type=MESH,
        )

    def travels(way, hop, h):
        return hop > 0 or h == way

    def ring_step(late, hop):
        far = reach - hop
        for way in range(2):
            h = way if late == 0 else 1 - way
            at = lax.rem(z + (far if way == 0 else nz - far), nz)
            val = own_part(at, h)
            if hop > late:
                ring_copy(way, hop - 1, h).wait_recv()
                val = val + ring_recv[way, hop - 1, h].astype(F32)
            ring_send[way, hop, h] = val.astype(BF16)
            ring_copy(way, hop, h).start()

    ring_steps = [(late, hop) for hop in range(1, reach) for late in (1, 0) if hop > late]

    def ring_next():
        if ring_steps:
            ring_step(*ring_steps.pop(0))

    def key_steps(e, wq, base, n, rows, use, shift=0):
        step = max(1, min(n, KG // rows))

        def one(j, _):
            j = lax.rem(j + shift, n // step)
            first = base + j * step
            at = pl.ds(pl.multiple_of(first * rows, rows), step * rows)
            k = jnp.dot(e[at, :], wq[...], preferred_element_type=F32)
            use(j, step, k.reshape(step, rows, width))
            return 0

        lax.fori_loop(0, n // step, one, 0)

    ring_step(0, 0)
    if reach > 1:
        ring_step(1, 1)

    def send_rows(j, step, k):
        k = k.astype(BF16)
        for h in range(step):
            p = j * step + h
            d_send[p] = k[h]

            @pl.when(p != qi)
            def _():
                x_d.start_to(p)

    lines = 4 if nq >= 16 else 1
    line = qi // (nq // lines)
    key_steps(e_s, wq_s, 0, nq, dest, send_rows, line + 2)
    d_recv[qi] = d_send[qi]
    ring_next()

    def core_copy(ch):
        return remote(core_send.at[ch], core_recv.at[ch], 8, ch, ch, "query", twin)

    def send_twin(j, step, k):
        k = k.astype(BF16)
        for h in range(step):
            ch = j * step + h
            core_send[ch] = k[h]
            core_copy(ch).start()

    def c_copy(ch, slot):
        return remote(c_send.at[ch], c_recv.at[slot], 9, ch, slot, "query", ch * 2 + core)

    def send_chip(j, step, k):
        for h in range(step):
            ch = j * step + h
            core_copy(ch).wait_recv()
            c_send[ch] = (k[h] + core_recv[ch].astype(F32)).astype(BF16)

            @pl.when(ch != chip)
            def _():
                c_copy(ch, chip).start()

    key_steps(e_i, wq_i, twin_base, nchip, sl, send_twin)
    ring_next()
    key_steps(e_i, wq_i, core * nchip, nchip, sl, send_chip)
    c_recv[chip] = c_send[chip]
    while ring_steps:
        ring_next()

    def table_part(j):
        many = nq // lines
        first = lax.rem(line + j, lines) * many

        def arrived(k, _):
            @pl.when(first + k != qi)
            def _():
                x_d.wait_from(first + k)

            return 0

        lax.fori_loop(0, many, arrived, 0)
        at = pl.ds(pl.multiple_of(first * dest, dest), many * dest)
        got = d_recv[pl.ds(first, many)].reshape(many * dest, width)
        part = jnp.dot(hot[:, at], got, preferred_element_type=F32)
        if j > 0:
            part = part + tgrad[...]
        if j < lines - 1:
            tgrad[...] = part
        else:
            tg_ref[...] = part.reshape(nblk, per, width).astype(BF16)

    for j in range(lines // 2):
        table_part(j)
    sums = []
    for h in range(2):
        val = own_part(z, h)
        for way in range(2):
            if travels(way, reach - 1, h):
                ring_copy(way, reach - 1, h).wait_recv()
                val = val + ring_recv[way, reach - 1, h].astype(F32)
        sums.append(val)
    half_send[...] = jnp.where(xh == 0, sums[1], sums[0]).astype(BF16)
    half = remote(half_send, half_recv, 10, 0, 0, "item", mirror)
    half.start()
    half_mine[...] = jnp.where(xh == 0, sums[0], sums[1]) - SCALE * r_mine
    for j in range(lines // 2, lines):
        table_part(j)
    half.wait_recv()
    qg_ref[...] = (half_mine[...] + half_recv[...].astype(F32)).astype(BF16)

    other_chips(lambda ch: c_copy(ch, ch).wait_recv())
    total = c_recv[0].astype(F32)
    for ch in range(1, nchip):
        total = total + c_recv[ch].astype(F32)
    pg_ref[...] = (total - SCALE * q_mine).astype(BF16)

    for x in (x_cnt, x_log, x_key, x_d):
        x.wait_send()
    row_twin().wait_send()
    other_z(lambda zz: stat_copy(zz, z).wait_send())
    stat_pair.wait_send()
    half.wait_send()
    for hop in range(reach):
        for h in range(2):
            for way in range(2):
                if travels(way, hop, h):
                    ring_copy(way, hop, h).wait_send()

    def sent(ch):
        row_out(ch).wait_send()
        row_pass(ch).wait_send()
        c_copy(ch, chip).wait_send()

    other_chips(sent)

    def sent_twin(ch, _):
        core_copy(ch).wait_send()
        return 0

    lax.fori_loop(0, nchip, sent_twin, 0)


def hand_over(*refs):
    for j in range(4):
        refs[4 + j][...] = refs[j][...]


def solution(mesh):
    nq, ni = mesh.shape["query"], mesh.shape["item"]

    def step(queries, table, counts, lists, positives, positive_rows):
        nblk, block, width = table.shape
        nqry, sl, cap = queries.shape[0], positive_rows.shape[0], lists.shape[2]
        per = block // nq
        dest = cap * per
        nk_s, nk_i = nq * dest, nq * sl
        most = max(nk_s, nk_i)
        reach = ni // 4
        vm, dma = pltpu.VMEM, pltpu.SemaphoreType.DMA
        whole = pl.BlockSpec(memory_space=vm)
        loss, qg, pg, tg = pl.pallas_call(
            functools.partial(kernel, nq, ni),
            out_shape=(
                vm((1, sl), F32),
                vm((sl, width), BF16),
                vm((sl, width), BF16),
                vm((nblk, per, width), BF16),
            ),
            in_specs=[pl.BlockSpec(memory_space=pl.ANY)] * 6,
            out_specs=[whole] * 4,
            scratch_shapes=[
                vm((nblk, block, width), BF16),
                vm((nqry, width), BF16),
                vm((nblk, block), I32),
                pltpu.SMEM((1, 1, cap), I32),
                vm((ni, 128), I32),
                vm((sl, width), BF16),
                vm((nq, dest, width), BF16),
                vm((nq, sl, width), BF16),
                vm((nq, dest, 128), F32),
                vm((nq, sl, 128), F32),
                vm((nk_s, nqry), BF16),
                vm((nk_i, nqry), BF16),
                vm((most, TQ), F32),
                vm((most, TQ), F32),
                vm((8, TQ), F32),
                vm((8, TQ), F32),
                vm((1, nqry), F32),
                vm((1, nqry), F32),
                vm((1, nqry), F32),
                vm((1, nqry), F32),
                vm((nqry, width), F32),
                vm((nqry, width), F32),
                vm((nqry, width), BF16),
                vm((nqry, width), BF16),
                vm((128, 128), F32),
                vm((ni, 1, sl), F32),
                vm((ni, 1, sl), F32),
                vm((1, sl), F32),
                vm((nq, 1, sl), F32),
                vm((1, dest), I32),
                vm((nq, 1, dest), I32),
                vm((2 * ni, sl), F32),
                vm((2 * ni, sl), F32),
                vm((2, ni, sl), F32),
                vm((ni // 2, 2, ni, sl), F32),
                vm((2, ni, sl), F32),
                vm((2, ni, sl), F32),
                vm((ni, sl), F32),
                vm((2, reach, 2, sl, width), BF16),
                vm((2, reach, 2, sl, width), BF16),
                vm((sl, width), BF16),
                vm((sl, width), BF16),
                vm((sl, width), F32),
                vm((nblk * per, width), F32),
                vm((nq // 2, sl, width), BF16),
                vm((nq // 2, sl, width), BF16),
                vm((nq // 2, sl, width), BF16),
                vm((nq // 2, sl, width), BF16),
                vm((nq, dest, width), BF16),
                vm((nq, dest, width), BF16),
                vm((nblk * per, nq * dest), BF16),
                dma((6,)),
                dma((11, max(nq, ni))),
                dma((11, max(nq, ni))),
                dma((2, reach, 2)),
                dma((2, reach, 2)),
            ],
            compiler_params=pltpu.CompilerParams(
                collective_id=0, has_side_effects=True, vmem_limit_bytes=60 << 20
            ),
        )(table, queries, counts, lists, positives.reshape(-1, 128), positive_rows)
        parts = (loss, qg, pg, tg)
        loss, qg, pg, tg = pl.pallas_call(
            hand_over,
            out_shape=tuple(jax.ShapeDtypeStruct(a.shape, a.dtype) for a in parts),
            in_specs=[whole] * 4,
            out_specs=[whole] * 4,
        )(*(pltpu.with_memory_space_constraint(a, vm) for a in parts))
        return loss.reshape(sl), qg, pg, tg

    return jax.shard_map(
        step,
        mesh=mesh,
        in_specs=(
            P("query", None),
            P("item", None, None),
            P("item", None),
            P("query", "item", None),
            P("query"),
            P(("query", "item"), None),
        ),
        out_specs=(
            P(("query", "item")),
            P(("query", "item"), None),
            P(("query", "item"), None),
            P("item", "query", None),
        ),
        check_vma=False,
    )
```

```python
import functools

import jax
import jax.numpy as jnp
from jax import lax
from jax.experimental import pallas as pl
from jax.experimental.pallas import tpu as pltpu
from jax.sharding import PartitionSpec as P

MESH = pl.DeviceIdType.MESH
F32, BF16, I32 = jnp.float32, jnp.bfloat16, jnp.int32
LOG2E = 1.4426950408889634
LN2 = 0.6931471805599453
SCALE = 0.125
TQ = 256
KC = 256
KG = 512


def iota(shape, dim):
    return lax.broadcasted_iota(I32, shape, dim)


def kernel(
    nq,
    ni,
    table_hbm,
    q_hbm,
    counts_hbm,
    lists_hbm,
    pos_hbm,
    rows_hbm,
    loss_ref,
    qg_ref,
    pg_ref,
    tg_ref,
    table_v,
    q_ref,
    counts_ref,
    lists_ref,
    pos_ref,
    rows_ref,
    keys_s,
    keys_i,
    lc_s,
    lc_i,
    e_s,
    e_i,
    s_a,
    s_b,
    m_a,
    m_b,
    mx_s,
    mx_i,
    sm_s,
    sm_i,
    g_s,
    g_i,
    wq_s,
    wq_i,
    tp,
    cnt_send,
    cnt_recv,
    log_send,
    log_recv,
    key_send,
    key_recv,
    row_mx,
    row_sm,
    stat_send,
    stat_recv,
    pair_send,
    pair_recv,
    lse_rows,
    ring_send,
    ring_recv,
    half_send,
    half_recv,
    half_mine,
    tgrad,
    core_send,
    core_recv,
    c_send,
    c_recv,
    d_send,
    d_recv,
    hot,
    in_sem,
    ssem,
    rsem,
    ring_ssem,
    ring_rsem,
):
    qi, ii = lax.axis_index("query"), lax.axis_index("item")
    nblk, block, width = table_v.shape
    cap = lists_ref.shape[2]
    nqry = q_ref.shape[0]
    sl = rows_ref.shape[0]
    per = block // nq
    dest = cap * per
    nk = keys_s.shape[0]
    ntile = nqry // TQ
    nchip, nz = nq // 2, ni // 2
    chip, core = qi // 2, lax.rem(qi, 2)
    twin = qi + 1 - 2 * core
    z, xh = ii // 2, lax.rem(ii, 2)
    mirror = ii + 1 - 2 * xh
    reach = nz // 2

    def to(axis, me, n, src, dst, x):
        def copy(peer, slot):
            return pltpu.make_async_remote_copy(
                src_ref=src(peer),
                dst_ref=dst.at[slot],
                send_sem=ssem.at[x, peer],
                recv_sem=rsem.at[x, slot],
                device_id={axis: peer},
                device_id_type=MESH,
            )

        def each(act):
            def step(off, _):
                act(lax.rem(me + off, n))
                return 0

            lax.fori_loop(1, n, step, 0)

        class X:
            start_to = staticmethod(lambda p: copy(p, me).start())
            start = staticmethod(lambda: each(X.start_to))
            wait_from = staticmethod(lambda p: copy(p, p).wait_recv())
            wait_recv = staticmethod(lambda: each(lambda p: copy(p, p).wait_recv()))
            wait_send = staticmethod(lambda: each(lambda p: copy(p, me).wait_send()))

        return X

    x_cnt = to("item", ii, ni, lambda p: cnt_send.at[p], cnt_recv, 1)
    x_log = to("query", qi, nq, lambda p: log_send, log_recv, 2)
    x_key = to("query", qi, nq, lambda p: key_send, key_recv, 3)
    x_d = to("query", qi, nq, lambda p: d_send.at[p], d_recv, 6)

    def remote(src, dst, x, s_at, r_at, axis, peer):
        return pltpu.make_async_remote_copy(
            src_ref=src,
            dst_ref=dst,
            send_sem=ssem.at[x, s_at],
            recv_sem=rsem.at[x, r_at],
            device_id={axis: peer},
            device_id_type=MESH,
        )

    def other_chips(act):
        def step(off, _):
            act(lax.rem(chip + off, nchip))
            return 0

        lax.fori_loop(1, nchip, step, 0)

    own_slot, twin_base = core * nchip + chip, (1 - core) * nchip

    def row_out(ch):
        return remote(rows_ref, keys_i.at[own_slot], 0, ch, own_slot, "query", ch * 2 + core)

    def row_twin():
        return remote(rows_ref, keys_i.at[own_slot], 7, chip, own_slot, "query", twin)

    def row_pass(ch):
        at = core * nchip + ch
        return remote(keys_i.at[at], keys_i.at[at], 7, ch, at, "query", twin)

    def row_from_twin(ch):
        at = twin_base + ch
        return remote(keys_i.at[at], keys_i.at[at], 7, ch, at, "query", twin)

    barrier = pltpu.get_barrier_semaphore()

    def greet(axis, me, n):
        def step(off, _):
            pl.semaphore_signal(
                barrier, inc=1, device_id={axis: lax.rem(me + off, n)}, device_id_type=MESH
            )
            return 0

        lax.fori_loop(1, n, step, 0)

    greet("query", qi, nq)
    greet("item", ii, ni)
    loads = [
        pltpu.make_async_copy(a, b, in_sem.at[j])
        for j, (a, b) in enumerate(
            (
                (rows_hbm, rows_ref),
                (lists_hbm, lists_ref),
                (counts_hbm, counts_ref),
                (pos_hbm, pos_ref),
                (table_hbm, table_v),
                (q_hbm, q_ref),
            )
        )
    ]
    for load in loads:
        load.start()
    loads[0].wait()
    keys_i[own_slot] = rows_ref[...]
    pl.semaphore_wait(barrier, nq + ni - 2)
    other_chips(lambda ch: row_out(ch).start())
    row_twin().start()
    for load in loads[1:4]:
        load.wait()

    cnt = counts_ref[...]
    halves = jnp.concatenate([cnt >> 8, cnt & 255], axis=0).astype(F32)
    by_row = jnp.transpose(halves).astype(BF16)

    wide = min(4, ni)
    for o in range(0, ni, wide):
        p = jnp.concatenate([pos_ref[o + j : o + j + 1, :] for j in range(wide)], axis=1)
        blk = (p >> 7) - ii * nblk
        one = (iota((nblk, wide * sl), 0) == blk).astype(F32)
        both = jnp.concatenate([one * 256.0, one], axis=0).astype(BF16)
        found = jnp.dot(by_row, both, preferred_element_type=F32)
        found = jnp.where(iota((block, wide * sl), 0) == (p & (block - 1)), found, 0.0)
        found = jnp.sum(found, axis=0, keepdims=True)
        for j in range(wide):
            cnt_send[o + j] = found[:, j * sl : (j + 1) * sl]
    cnt_recv[ii] = cnt_send[ii]
    x_cnt.start()

    lane = iota((1, dest), 1)
    lane_c, lane_r = lane // per, lane % per
    lane_key = lane_r
    for c in range(cap):
        lane_key = lane_key + jnp.where(lane_c == c, lists_ref[0, 0, c] * per, 0)
    key_send[...] = lane_key
    key_recv[qi] = lane_key
    x_key.start()

    tp[...] = jnp.zeros_like(tp)
    for c in range(cap):
        row = counts_ref[pl.ds(lists_ref[0, 0, c], 1), :].astype(F32)
        tp[c : c + 1, :] = jnp.log(row) * LOG2E
    cols = jnp.transpose(tp[...])
    for c in range(cap):
        col = jnp.broadcast_to(cols[:, c : c + 1], (block, 128))
        lc_s[:, c * per : (c + 1) * per, :] = col.reshape(nq, per, 128)
    loads[4].wait()
    pair = max(1, 16 // per)
    for c in range(0, cap, pair):
        parts = [
            table_v[lists_ref[0, 0, c + j]].astype(F32).reshape(nq, per, width)
            for j in range(pair)
        ]
        both = jnp.concatenate(parts, axis=1) if pair > 1 else parts[0]
        keys_s[:, c * per : (c + pair) * per, :] = both.astype(BF16)

    def chunks(ref, size):
        n, rows = ref.shape[0], ref.shape[1]
        step = max(1, min(n, size // rows))
        return [(j, j + step) for j in range(0, n, step)], rows

    def scores(keys, lc, e, mx, sm, between=None):
        spans, rows = chunks(keys, KC)

        def tile_of(t):
            return q_ref[pl.ds(pl.multiple_of(t * TQ, TQ), TQ), :]

        def both(t_new, s_new, m_new, t_old, s_old, m_old):
            if t_new is not None:
                q = tile_of(t_new)
                m8 = jnp.full((8, TQ), -jnp.inf, F32)
            if t_old is not None:
                top = jnp.max(m_old[...], axis=0, keepdims=True)
                at = pl.ds(pl.multiple_of(t_old * TQ, TQ), TQ)
                s8 = jnp.zeros((8, TQ), F32)
            for lo, hi in spans:
                n = (hi - lo) * rows
                if t_new is not None:
                    k = keys[lo:hi].reshape(n, width)
                    d = lax.dot_general(
                        k, q, (((1,), (1,)), ((), ())), preferred_element_type=F32
                    )
                    c = lc[lo:hi].reshape(n, 128)
                    s = d * (SCALE * LOG2E) - jnp.concatenate([c] * (TQ // 128), axis=1)
                    s_new[lo * rows : hi * rows, :] = s
                    m8 = jnp.maximum(m8, jnp.max(s.reshape(n // 8, 8, TQ), axis=0))
                if t_old is not None:
                    x = jnp.exp2(s_old[lo * rows : hi * rows, :] - top)
                    s8 = s8 + jnp.sum(x.reshape(n // 8, 8, TQ), axis=0)
                    e[lo * rows : hi * rows, at] = x.astype(BF16)
            if t_new is not None:
                m_new[...] = m8
            if t_old is not None:
                mx[:, at] = top
                sm[:, at] = jnp.sum(s8, axis=0, keepdims=True)

        both(0, s_a, m_a, None, None, None)

        def pair_of_tiles(u, _):
            both(2 * u + 1, s_b, m_b, 2 * u, s_a, m_a)
            both(2 * u + 2, s_a, m_a, 2 * u + 1, s_b, m_b)
            return 0

        lax.fori_loop(0, ntile // 2 - 1, pair_of_tiles, 0)
        if between is not None:
            between()
        both(ntile - 1, s_b, m_b, ntile - 2, s_a, m_a)
        both(None, None, None, ntile - 1, s_b, m_b)

    def query_grads(keys, e, g, half):
        n = keys.shape[0] * keys.shape[1]
        at = slice(half * nqry // 2, (half + 1) * nqry // 2)
        g[at, :] = lax.dot_general(
            e[:, at],
            keys[...].reshape(n, width),
            (((0,), (0,)), ((), ())),
            preferred_element_type=F32,
        )

    loads[5].wait()

    def log_counts():
        x_cnt.wait_recv()
        total = cnt_recv[0]
        for o in range(1, ni):
            total = total + cnt_recv[o]
        mine_logc = jnp.log(total).astype(BF16).astype(F32)
        log_send[...] = mine_logc
        log_recv[qi] = mine_logc
        x_log.start()

    scores(keys_s, lc_s, e_s, mx_s, sm_s, log_counts)

    def pass_on(ch):
        remote(
            keys_i.at[core * nchip + ch],
            keys_i.at[core * nchip + ch],
            0,
            ch,
            core * nchip + ch,
            "query",
            ch * 2 + core,
        ).wait_recv()
        row_pass(ch).start()

    other_chips(pass_on)

    x_key.wait_recv()
    for g in range(nq):
        want = iota((nblk * per, dest), 0)
        hot[:, g * dest : (g + 1) * dest] = jnp.where(
            want == key_recv[g], 1.0, 0.0
        ).astype(BF16)

    query_grads(keys_s, e_s, g_s, 0)
    x_log.wait_recv()
    for g in range(nq):
        tp[g : g + 1, :] = log_recv[g] * LOG2E
    cols = jnp.transpose(tp[...])
    for g in range(nq):
        lc_i[(g % 2) * nchip + g // 2] = jnp.broadcast_to(cols[:, g : g + 1], (sl, 128))

    def from_twin(ch, _):
        row_from_twin(ch).wait_recv()
        return 0

    lax.fori_loop(0, nchip, from_twin, 0)
    scores(keys_i, lc_i, e_i, mx_i, sm_i)

    for o in range(ni):
        at = slice(o * sl, (o + 1) * sl)
        row_mx[o : o + 1, :] = mx_s[:, at]
        row_mx[ni + o : ni + o + 1, :] = mx_i[:, at]
        row_sm[o : o + 1, :] = sm_s[:, at]
        row_sm[ni + o : ni + o + 1, :] = sm_i[:, at]

    def met(pairs):
        top = pairs[0][0]
        for m, _ in pairs[1:]:
            top = jnp.maximum(top, m)
        return top, sum(v * jnp.exp2(m - top) for m, v in pairs)

    top, part = met(
        [(row_mx[j : j + ni, :], row_sm[j : j + ni, :]) for j in (0, ni)]
    )
    stat_send[0], stat_send[1] = top, part
    stat_recv[z, 0], stat_recv[z, 1] = top, part

    def stat_copy(zz, slot):
        return remote(stat_send, stat_recv.at[slot], 4, zz, slot, "item", zz * 2 + xh)

    def other_z(act):
        def step(off, _):
            act(lax.rem(z + off, nz))
            return 0

        lax.fori_loop(1, nz, step, 0)

    other_z(lambda zz: stat_copy(zz, z).start())
    query_grads(keys_s, e_s, g_s, 1)
    other_z(lambda zz: stat_copy(zz, zz).wait_recv())
    top, part = met([(stat_recv[j, 0], stat_recv[j, 1]) for j in range(nz)])
    pair_send[0], pair_send[1] = top, part
    stat_pair = remote(pair_send, pair_recv, 5, 0, 0, "item", mirror)
    stat_pair.start()
    query_grads(keys_i, e_i, g_i, 0)
    query_grads(keys_i, e_i, g_i, 1)
    stat_pair.wait_recv()
    top, part = met([(pair_send[0], pair_send[1]), (pair_recv[0], pair_recv[1])])
    lse_rows[...] = top + jnp.log(part) * LOG2E

    mine = pl.ds(pl.multiple_of(ii * sl, sl), sl)
    q_mine = q_ref[mine, :].astype(F32)
    r_mine = rows_ref[...].astype(F32)
    label = SCALE * jnp.sum(q_mine * r_mine, axis=1, keepdims=True)
    label = jnp.sum(
        jnp.where(iota((sl, sl), 0) == iota((sl, sl), 1), label, 0.0), axis=0, keepdims=True
    )
    loss_ref[...] = lse_rows[pl.ds(ii, 1), :] * LN2 - (label - log_send[...])

    for j in (0, ni):
        tp[j : j + ni, :] = jnp.exp2(row_mx[j : j + ni, :] - lse_rows[...]) * SCALE
    cols = jnp.transpose(tp[...])
    for o in range(ni):
        at = slice(o * sl, (o + 1) * sl)
        w_s, w_i = cols[:, o : o + 1], cols[:, ni + o : ni + o + 1]
        q = q_ref[at, :].astype(F32)
        wq_s[at, :] = (q * w_s).astype(BF16)
        wq_i[at, :] = (q * w_i).astype(BF16)
        g_s[at, :] = g_s[at, :] * w_s + g_i[at, :] * w_i

    def own_part(zz, h):
        at = pl.multiple_of((zz * 2 + h) * sl, sl)
        return g_s[pl.ds(at, sl), :]

    def ring_copy(way, hop, h):
        to_z = lax.rem(z + (1 if way == 0 else nz - 1), nz)
        return pltpu.make_async_remote_copy(
            src_ref=ring_send.at[way, hop, h],
            dst_ref=ring_recv.at[way, hop, h],
            send_sem=ring_ssem.at[way, hop, h],
            recv_sem=ring_rsem.at[way, hop, h],
            device_id={"item": to_z * 2 + xh},
            device_id_type=MESH,
        )

    def travels(way, hop, h):
        return hop > 0 or h == way

    def ring_step(late, hop):
        far = reach - hop
        for way in range(2):
            h = way if late == 0 else 1 - way
            at = lax.rem(z + (far if way == 0 else nz - far), nz)
            val = own_part(at, h)
            if hop > late:
                ring_copy(way, hop - 1, h).wait_recv()
                val = val + ring_recv[way, hop - 1, h].astype(F32)
            ring_send[way, hop, h] = val.astype(BF16)
            ring_copy(way, hop, h).start()

    ring_steps = [(late, hop) for hop in range(1, reach) for late in (1, 0) if hop > late]

    def ring_next():
        if ring_steps:
            ring_step(*ring_steps.pop(0))

    def key_steps(e, wq, base, n, rows, use, shift=0):
        step = max(1, min(n, KG // rows))

        def one(j, _):
            j = lax.rem(j + shift, n // step)
            first = base + j * step
            at = pl.ds(pl.multiple_of(first * rows, rows), step * rows)
            k = jnp.dot(e[at, :], wq[...], preferred_element_type=F32)
            use(j, step, k.reshape(step, rows, width))
            return 0

        lax.fori_loop(0, n // step, one, 0)

    ring_step(0, 0)
    if reach > 1:
        ring_step(1, 1)

    def send_rows(j, step, k):
        k = k.astype(BF16)
        for h in range(step):
            p = j * step + h
            d_send[p] = k[h]

            @pl.when(p != qi)
            def _():
                x_d.start_to(p)

    lines = 4 if nq >= 16 else 1
    line = qi // (nq // lines)
    key_steps(e_s, wq_s, 0, nq, dest, send_rows, line + 2)
    d_recv[qi] = d_send[qi]
    ring_next()

    def core_copy(ch):
        return remote(core_send.at[ch], core_recv.at[ch], 8, ch, ch, "query", twin)

    def send_twin(j, step, k):
        k = k.astype(BF16)
        for h in range(step):
            ch = j * step + h
            core_send[ch] = k[h]
            core_copy(ch).start()

    def c_copy(ch, slot):
        return remote(c_send.at[ch], c_recv.at[slot], 9, ch, slot, "query", ch * 2 + core)

    def send_chip(j, step, k):
        for h in range(step):
            ch = j * step + h
            core_copy(ch).wait_recv()
            c_send[ch] = (k[h] + core_recv[ch].astype(F32)).astype(BF16)

            @pl.when(ch != chip)
            def _():
                c_copy(ch, chip).start()

    key_steps(e_i, wq_i, twin_base, nchip, sl, send_twin)
    ring_next()
    key_steps(e_i, wq_i, core * nchip, nchip, sl, send_chip)
    c_recv[chip] = c_send[chip]
    while ring_steps:
        ring_next()

    def table_part(j):
        many = nq // lines
        first = lax.rem(line + j, lines) * many

        def arrived(k, _):
            @pl.when(first + k != qi)
            def _():
                x_d.wait_from(first + k)

            return 0

        lax.fori_loop(0, many, arrived, 0)
        at = pl.ds(pl.multiple_of(first * dest, dest), many * dest)
        got = d_recv[pl.ds(first, many)].reshape(many * dest, width)
        part = jnp.dot(hot[:, at], got, preferred_element_type=F32)
        if j > 0:
            part = part + tgrad[...]
        if j < lines - 1:
            tgrad[...] = part
        else:
            tg_ref[...] = part.reshape(nblk, per, width).astype(BF16)

    for j in range(lines // 4):
        table_part(j)
    sums = []
    for h in range(2):
        val = own_part(z, h)
        for way in range(2):
            if travels(way, reach - 1, h):
                ring_copy(way, reach - 1, h).wait_recv()
                val = val + ring_recv[way, reach - 1, h].astype(F32)
        sums.append(val)
    half_send[...] = jnp.where(xh == 0, sums[1], sums[0]).astype(BF16)
    half = remote(half_send, half_recv, 10, 0, 0, "item", mirror)
    half.start()
    half_mine[...] = jnp.where(xh == 0, sums[0], sums[1]) - SCALE * r_mine
    for j in range(lines // 4, lines):
        table_part(j)
    half.wait_recv()
    qg_ref[...] = (half_mine[...] + half_recv[...].astype(F32)).astype(BF16)

    other_chips(lambda ch: c_copy(ch, ch).wait_recv())
    total = c_recv[0].astype(F32)
    for ch in range(1, nchip):
        total = total + c_recv[ch].astype(F32)
    pg_ref[...] = (total - SCALE * q_mine).astype(BF16)

    for x in (x_cnt, x_log, x_key, x_d):
        x.wait_send()
    row_twin().wait_send()
    other_z(lambda zz: stat_copy(zz, z).wait_send())
    stat_pair.wait_send()
    half.wait_send()
    for hop in range(reach):
        for h in range(2):
            for way in range(2):
                if travels(way, hop, h):
                    ring_copy(way, hop, h).wait_send()

    def sent(ch):
        row_out(ch).wait_send()
        row_pass(ch).wait_send()
        c_copy(ch, chip).wait_send()

    other_chips(sent)

    def sent_twin(ch, _):
        core_copy(ch).wait_send()
        return 0

    lax.fori_loop(0, nchip, sent_twin, 0)


def hand_over(*refs):
    for j in range(4):
        refs[4 + j][...] = refs[j][...]


def solution(mesh):
    nq, ni = mesh.shape["query"], mesh.shape["item"]

    def step(queries, table, counts, lists, positives, positive_rows):
        nblk, block, width = table.shape
        nqry, sl, cap = queries.shape[0], positive_rows.shape[0], lists.shape[2]
        per = block // nq
        dest = cap * per
        nk_s, nk_i = nq * dest, nq * sl
        most = max(nk_s, nk_i)
        reach = ni // 4
        vm, dma = pltpu.VMEM, pltpu.SemaphoreType.DMA
        whole = pl.BlockSpec(memory_space=vm)
        loss, qg, pg, tg = pl.pallas_call(
            functools.partial(kernel, nq, ni),
            out_shape=(
                vm((1, sl), F32),
                vm((sl, width), BF16),
                vm((sl, width), BF16),
                vm((nblk, per, width), BF16),
            ),
            in_specs=[pl.BlockSpec(memory_space=pl.ANY)] * 6,
            out_specs=[whole] * 4,
            scratch_shapes=[
                vm((nblk, block, width), BF16),
                vm((nqry, width), BF16),
                vm((nblk, block), I32),
                pltpu.SMEM((1, 1, cap), I32),
                vm((ni, 128), I32),
                vm((sl, width), BF16),
                vm((nq, dest, width), BF16),
                vm((nq, sl, width), BF16),
                vm((nq, dest, 128), F32),
                vm((nq, sl, 128), F32),
                vm((nk_s, nqry), BF16),
                vm((nk_i, nqry), BF16),
                vm((most, TQ), F32),
                vm((most, TQ), F32),
                vm((8, TQ), F32),
                vm((8, TQ), F32),
                vm((1, nqry), F32),
                vm((1, nqry), F32),
                vm((1, nqry), F32),
                vm((1, nqry), F32),
                vm((nqry, width), F32),
                vm((nqry, width), F32),
                vm((nqry, width), BF16),
                vm((nqry, width), BF16),
                vm((128, 128), F32),
                vm((ni, 1, sl), F32),
                vm((ni, 1, sl), F32),
                vm((1, sl), F32),
                vm((nq, 1, sl), F32),
                vm((1, dest), I32),
                vm((nq, 1, dest), I32),
                vm((2 * ni, sl), F32),
                vm((2 * ni, sl), F32),
                vm((2, ni, sl), F32),
                vm((ni // 2, 2, ni, sl), F32),
                vm((2, ni, sl), F32),
                vm((2, ni, sl), F32),
                vm((ni, sl), F32),
                vm((2, reach, 2, sl, width), BF16),
                vm((2, reach, 2, sl, width), BF16),
                vm((sl, width), BF16),
                vm((sl, width), BF16),
                vm((sl, width), F32),
                vm((nblk * per, width), F32),
                vm((nq // 2, sl, width), BF16),
                vm((nq // 2, sl, width), BF16),
                vm((nq // 2, sl, width), BF16),
                vm((nq // 2, sl, width), BF16),
                vm((nq, dest, width), BF16),
                vm((nq, dest, width), BF16),
                vm((nblk * per, nq * dest), BF16),
                dma((6,)),
                dma((11, max(nq, ni))),
                dma((11, max(nq, ni))),
                dma((2, reach, 2)),
                dma((2, reach, 2)),
            ],
            compiler_params=pltpu.CompilerParams(
                collective_id=0, has_side_effects=True, vmem_limit_bytes=60 << 20
            ),
        )(table, queries, counts, lists, positives.reshape(-1, 128), positive_rows)
        parts = (loss, qg, pg, tg)
        loss, qg, pg, tg = pl.pallas_call(
            hand_over,
            out_shape=tuple(jax.ShapeDtypeStruct(a.shape, a.dtype) for a in parts),
            in_specs=[whole] * 4,
            out_specs=[whole] * 4,
        )(*(pltpu.with_memory_space_constraint(a, vm) for a in parts))
        return loss.reshape(sl), qg, pg, tg

    return jax.shard_map(
        step,
        mesh=mesh,
        in_specs=(
            P("query", None),
            P("item", None, None),
            P("item", None),
            P("query", "item", None),
            P("query"),
            P(("query", "item"), None),
        ),
        out_specs=(
            P(("query", "item")),
            P(("query", "item"), None),
            P(("query", "item"), None),
            P("item", "query", None),
        ),
        check_vma=False,
    )
```
